32 devices in a mesh: member: 2 (over y), tile: 4 (over z), chan: 4 (over x, core).
Axes of the slice: x: 2, y: 2, z: 4, core: 2. Of those that a mesh axis runs over, the one named last changes fastest.
Arguments:
- latlon_grad: bfloat16 [128, 69, 128], P(('member', 'tile', 'chan')), parts along dimension 0, may hold values from -6 to 6
- remap_weight: bfloat16 [4096, 128, 128], P(('tile', 'chan')), may hold values from -0.5 to 0.5
- src_block: int32 [4096], P(('tile', 'chan')), may hold values from 0 to 3
- owner: int32 [4096], P(('tile', 'chan')), may hold values from 0 to 3, as said below
- target_half: int32 [4096], P(('tile', 'chan')), may hold values from 0 to 13
- live_count: int32 [16], P(('tile', 'chan')), may hold values from 96 to 256
- conv_weight: bfloat16 [9, 69, 256], replicated, may hold values from -0.125 to 0.125
- nbr_block: int32 [112, 4], P(('tile', 'chan')), may hold values from 0 to 111, as said below
- nbr_code: int32 [112, 4], P(('tile', 'chan')), may hold values from 0 to 7, as said below
Outputs:
- hidden_grad: bfloat16 [256, 224, 256], P(None, ('member', 'tile', 'chan')), parts along dimension 1
The draws below stay inside these ranges and needn't reach their ends.
There are 2 independent parts, one for each index of `member`. The reference program is written for one: setup_inputs(seed, part) draws one part's arguments, and reference() takes and returns one part's arrays. A program takes and returns all parts, laid end to end along the dimension named above; an argument that names none is the same for every part. Nothing has to cross between parts.
Inputs may be any that keep to these rules, and one draw needn't show every extreme that they name: `owner`: slots 64 m to 64 m + 63 of one device name one tile index, and different such runs of one device name different tile indices. The neighbour of a block of device index d (over tile+chan, d = block // 7) lies on device index d - 1, d or d + 1, taken cyclically; no block neighbours itself. The tables are symmetric: if nbr_block[g, s] = g' and nbr_code[g, s] = 2 s' + f, then nbr_block[g', s'] = g and nbr_code[g', s'] = 2 s + f. `nbr_code`: see nbr_block.
All inputs are finite; a program needn't handle non-finite values.
Results may differ from the reference program's by a relative error of at most 0.0058.
Values may be sent and summed in bfloat16 or wider, within the bound.
No kernel may reach another device: no remote copies, remote signals or barrier semaphores. Data moves between devices by JAX's collectives and lax.ppermute only.
A program may use at most 64 MiB of HBM per device.

```python
import jax
import jax.numpy as jnp
import numpy as np
from jax import lax

CH = 256
OUT_CH = 69
HALF = 128
TB = 7
LB_DEV = 4
E_DEV = 256
CELLS = 256
CAP = 64
DEVS = 16
NB = 112
LATBLOCKS = 64
ENTRIES = 4096
N_TILE = 4
N_CHAN = 4


def seam_tables(key):
    count = NB
    turn = jax.random.randint(jax.random.fold_in(key, 11), (count,), 0, 4)
    flip_east = jax.random.randint(jax.random.fold_in(key, 12), (count,), 0, 2)
    flip_north = jax.random.randint(jax.random.fold_in(key, 13), (count,), 0, 2)
    block = jnp.arange(count, dtype=jnp.int32)
    north = (block + TB) % count
    south = (block - TB) % count
    east = (block + 1) % count
    west = (block - 1) % count
    physical = jnp.stack([north, west, south, east], axis=1)
    physical_flip = jnp.stack([flip_north, flip_east[west], flip_north[south], flip_east], axis=1)
    sides = jnp.arange(4, dtype=jnp.int32)
    facing = (sides[None, :] - turn[:, None]) % 4
    neighbour = jnp.take_along_axis(physical, facing, axis=1)
    flip_bit = jnp.take_along_axis(physical_flip, facing, axis=1)
    other_side = ((facing + 2) % 4 + turn[neighbour]) % 4
    return (neighbour.astype(jnp.int32), (other_side * 2 + flip_bit).astype(jnp.int32))


def draw_nbr_block(key, part):
    shared = seam_tables(key)
    return shared[0]


def draw_nbr_code(key, part):
    shared = seam_tables(key)
    return shared[1]


def draw_owner(key, part):
    key = jax.random.fold_in(key, 3)
    chosen = jax.random.randint(jax.random.fold_in(key, 1), (), 0, N_TILE)
    device_keys = jax.random.split(jax.random.fold_in(key, 2), DEVS)
    orders = jax.vmap(lambda one_key: jax.random.permutation(one_key, N_TILE))(device_keys)
    leading = orders[:, 0]
    swapped = jnp.where(orders == chosen, leading[:, None], orders)
    swapped = swapped.at[:, 0].set(chosen)
    runs = jnp.arange(E_DEV, dtype=jnp.int32) // CAP
    return swapped[:, runs].reshape(DEVS * E_DEV).astype(jnp.int32)


def draw_live_count(key, part):
    key = jax.random.fold_in(key, 5)
    device = jnp.arange(DEVS, dtype=jnp.int32)
    tile_row = device // N_CHAN
    distance = (2 * tile_row - (N_TILE - 1)) ** 2
    spread = (N_TILE - 1) ** 2
    base_count = E_DEV // 2 + (E_DEV - E_DEV // 2) * distance // spread
    reach = max(1, E_DEV // 8)
    jitter = jax.random.randint(key, (DEVS,), 0, reach + 1) * (distance < spread).astype(jnp.int32)
    return (base_count - jitter).astype(jnp.int32)


def set_ends(values, stream_key, low, largest):
    extent = values.shape
    index_at = [jax.random.randint(jax.random.fold_in(stream_key, axis), (), 0, extent[axis]) for axis in range(len(extent))]
    values = values.at[tuple(index_at)].set(low)
    longest = extent.index(max(extent))
    index_at[longest] = (index_at[longest] + 1) % extent[longest]
    return values.at[tuple(index_at)].set(largest)


def steps_of(key, dims, pieces, least, top_value):
    factor_of, own = 1.0, jax.random.fold_in(key, 6)
    for dim, blocks in pieces:
        draws = jnp.exp(jax.random.uniform(jax.random.fold_in(own, dim), (blocks,), jnp.float32, least / len(pieces), top_value / len(pieces)))
        factor_of = factor_of * jnp.repeat(draws, dims[dim] // blocks).reshape([-1 if axis == dim else 1 for axis in range(len(dims))])
    return factor_of


def scatter_about(rng, shape, scale, limit, cuts=(), kind=jnp.bfloat16):
    values = jax.random.normal(rng, shape, jnp.float32) * scale
    if len(cuts) > 0:
        values = steps_of(rng, shape, cuts, -0.22, 0.18) * values
    return jnp.clip(values, min=-limit, max=limit).astype(kind)


def setup_inputs(seed: int = 0, part: int = 0) -> dict:
    seeds = jax.random.split(jax.random.key(seed), 10)
    part_keys = jax.random.split(jax.random.fold_in(seeds[9], part), 10)
    return {
        "latlon_grad": scatter_about(part_keys[0], (LATBLOCKS, OUT_CH, HALF), 1.0, 6.0, ((0, 16),)),
        "remap_weight": scatter_about(seeds[1], (ENTRIES, HALF, HALF), HALF ** -0.5, 0.5, ((0, 16),)),
        "src_block": set_ends(jax.random.randint(seeds[2], (ENTRIES,), 0, LB_DEV), jax.random.fold_in(seeds[2], 1), 0, LB_DEV - 1).astype(jnp.int32),
        "owner": draw_owner(jax.random.fold_in(seeds[9], 71), part),
        "target_half": set_ends(jax.random.randint(seeds[4], (ENTRIES,), 0, 2 * TB), jax.random.fold_in(seeds[4], 1), 0, (2 * TB) - 1).astype(jnp.int32),
        "live_count": draw_live_count(jax.random.fold_in(seeds[9], 71), part),
        "conv_weight": scatter_about(seeds[6], (9, OUT_CH, CH), (9 * CH) ** -0.5, 0.125),
        "nbr_block": draw_nbr_block(jax.random.fold_in(seeds[9], 71), part),
        "nbr_code": draw_nbr_code(jax.random.fold_in(seeds[9], 71), part),
    }


SHIFTS = tuple(18 * (offset // 3 - 1) + (offset % 3 - 1) for offset in range(9))


def rim_cells():
    top_side = [position + 1 for position in range(16)]
    left_side = [18 * (position + 1) for position in range(16)]
    bottom_side = [306 + position + 1 for position in range(16)]
    right_side = [18 * (position + 1) + 17 for position in range(16)]
    return np.array(top_side + left_side + bottom_side + right_side, dtype=np.int32)


def framed(cotangent):
    channels, blocks, cell_count = cotangent.shape
    square = cotangent.reshape(channels, blocks, 16, 16)
    return jnp.pad(square, ((0, 0), (0, 0), (1, 1), (1, 1))).reshape(channels, blocks, 324)


def rolled_stack(framed_grid):
    return jnp.stack([jnp.roll(framed_grid, offset_cells, axis=2) for offset_cells in SHIFTS])


def finish(pad_grad, incoming):
    channels, blocks, cell_count = pad_grad.shape
    inner_part = pad_grad.reshape(channels, blocks, 18, 18)[:, :, 1:17, 1:17]
    extra_rims = incoming.reshape(channels, blocks, 4, 16)
    inner_part = inner_part.at[:, :, 0, :].add(extra_rims[:, :, 0]).at[:, :, :, 0].add(extra_rims[:, :, 1])
    inner_part = inner_part.at[:, :, 15, :].add(extra_rims[:, :, 2]).at[:, :, :, 15].add(extra_rims[:, :, 3])
    return inner_part.reshape(channels, blocks, 256).astype(jnp.bfloat16)


def reference(latlon_grad, remap_weight, src_block, owner, target_half, live_count, conv_weight, nbr_block, nbr_code):
    devices = N_TILE * N_CHAN
    grads = latlon_grad.reshape(devices, LB_DEV, OUT_CH, HALF)
    weights = remap_weight.reshape(devices, E_DEV, HALF, HALF)
    sources = src_block.reshape(devices, E_DEV)
    owners = owner.reshape(devices, E_DEV)
    targets = target_half.reshape(devices, E_DEV)
    slot_number = jnp.arange(E_DEV, dtype=jnp.int32)

    def remap_device(half_totals, device_items):
        device_index, grad_rows, weight_rows, source, owner_row, target = device_items
        live_mask = (slot_number < live_count[device_index]).astype(jnp.float32)
        picked = jnp.take(grad_rows, source, axis=0).astype(jnp.float32)
        product = jnp.einsum("eoa,eab->eob", picked, weight_rows.astype(jnp.float32))
        product = (product * live_mask[:, None, None]).astype(jnp.bfloat16)
        product = lax.optimization_barrier(product).astype(jnp.float32)
        slot_index = (owner_row * N_CHAN + device_index % N_CHAN) * (2 * TB) + target
        return half_totals.at[slot_index].add(product), None

    half_totals = jnp.zeros((2 * TB * devices, OUT_CH, HALF), jnp.float32)
    device_ids = jnp.arange(devices, dtype=jnp.int32)
    half_totals, unused = lax.scan(remap_device, half_totals, (device_ids, grads, weights, sources, owners, targets))
    half_grad = half_totals.astype(jnp.bfloat16)
    cotangent = half_grad.reshape(devices, TB, 2, OUT_CH, HALF).transpose(0, 3, 1, 2, 4).reshape(devices, OUT_CH, TB, CELLS)
    weight_float = conv_weight.astype(jnp.float32)
    rim_index = rim_cells()

    def rims_of(block_grad):
        rolled_frames = rolled_stack(framed(block_grad)).astype(jnp.float32)
        rim_float = jnp.einsum("kotr,koc->ctr", rolled_frames[:, :, :, rim_index], weight_float)
        return rim_float.astype(jnp.bfloat16)

    rim_values = lax.map(rims_of, cotangent)
    rim_values = rim_values.transpose(1, 0, 2, 3).reshape(CH, devices * TB * 64)
    position = jnp.arange(16, dtype=jnp.int32)
    flipped = nbr_code % 2
    along_edge = jnp.where(flipped[:, :, None] == 1, 15 - position, position)
    columns = ((nbr_block * 64 + (nbr_code // 2) * 16)[:, :, None] + along_edge).reshape(-1)
    incoming = jnp.take(rim_values, columns, axis=1).reshape(CH, devices, TB * 64).transpose(1, 0, 2)

    def finish_of(device_items):
        block_grad, incoming_rims = device_items
        rolled_frames = rolled_stack(framed(block_grad)).astype(jnp.float32)
        pad_grad = jnp.einsum("kotq,koc->ctq", rolled_frames, weight_float)
        return finish(pad_grad, incoming_rims.astype(jnp.float32))

    result = lax.map(finish_of, (cotangent, incoming))
    return result.transpose(1, 0, 2, 3).reshape(CH, devices * TB, CELLS)
```

```python
import jax
import jax.numpy as jnp
import numpy as np
from jax import lax
from jax.experimental import pallas as pl
from jax.experimental.pallas import tpu as pltpu
from jax.sharding import PartitionSpec as P

BF16 = jnp.bfloat16
F32 = jnp.float32
SIDE = 16
CELLS = SIDE * SIDE
LANES = 128
TAPS = 9
VMEM_LIMIT = 48 * 1024 * 1024


def edge_cell(side, position):
    return (
        position,
        SIDE * position,
        SIDE * (SIDE - 1) + position,
        SIDE * position + SIDE - 1,
    )[side]


def lane_order():
    edges = sorted({edge_cell(side, position) for side in range(4) for position in range(SIDE)})
    inner = [cell for cell in range(CELLS) if cell not in set(edges)]
    return edges + inner


def permutation_matrix():
    order = lane_order()
    matrix = np.zeros((CELLS, CELLS), np.float32)
    for lane, cell in enumerate(order):
        matrix[cell, lane] = 1
    return matrix


def shift_matrices():
    order = lane_order()
    matrix = np.zeros((TAPS, CELLS, CELLS), np.float32)
    for tap in range(TAPS):
        down, right = tap // 3 - 1, tap % 3 - 1
        for lane, cell in enumerate(order):
            row, column = cell // SIDE + down, cell % SIDE + right
            if 0 <= row < SIDE and 0 <= column < SIDE:
                matrix[tap, lane, row * SIDE + column] = 1
    return matrix


def edge_matrix():
    lane_of = {cell: lane for lane, cell in enumerate(lane_order())}
    matrix = np.zeros((LANES, 3, 2, 4, SIDE), np.float32)
    for shift in (-1, 0, 1):
        for half in range(2):
            for side in range(4):
                for position in range(SIDE):
                    if 0 <= position - shift < SIDE:
                        lane = lane_of[edge_cell(side, position - shift)]
                        matrix[64 * half + lane, shift + 1, half, side, position] = 1
    return matrix.reshape(LANES, 3 * LANES)


def place_matrix():
    matrix = np.zeros((4, SIDE, CELLS), np.float32)
    for side in range(4):
        for position in range(SIDE):
            matrix[side, position, edge_cell(side, position)] = 1
    return matrix.reshape(4 * SIDE, CELLS)


def rim_taps(side):
    return [((0 + d), 3 * d, 6 + d, 3 * d + 2)[side] for d in range(3)]


def constant(matrix):
    return jnp.asarray(matrix, BF16)


def whole(array):
    rank = array.ndim
    return pl.BlockSpec(array.shape, lambda *_: (0,) * rank)


def remap_runs(
    shifts, latlon_grad, remap_weight, src_block, owner, target_half, live_count, blocks, padded, kept
):
    slots, half = remap_weight.shape[:2]
    channels = latlon_grad.shape[1]
    sources = latlon_grad.shape[0]
    tiles = lax.axis_size("tile")
    run = slots // tiles
    chunk = min(16, run)
    chunks = run // chunk
    halves = 2 * blocks
    count = len(shifts)

    def kernel(*refs):
        live, src_in, tgt_in, own_in, grad_in, weight_in, perm_ref = refs[:7]
        refs = refs[7 + len(kept) :]
        out_refs, refs = refs[: 2 * count], refs[2 * count + len(kept) :]
        src, tgt, own, packed, grad, weight, total, small_sem, weight_sem = refs
        tile = lax.axis_index("tile")
        small = [
            pltpu.make_async_copy(source, target, small_sem.at[index])
            for index, (source, target) in enumerate(
                ((own_in, own), (src_in, src), (tgt_in, tgt), (grad_in, packed))
            )
        ]
        for copy in small:
            copy.start()
        small[0].wait()
        firsts = []
        copies = []
        for place, shift in enumerate(shifts):
            wanted = lax.rem(tile + shift, tiles)
            found = jnp.int32(0)
            for index in range(tiles):
                found = found + jnp.where(own[index * run] == wanted, index, 0)
            firsts.append(found * run)
            for part in range(chunks):
                copies.append(
                    pltpu.make_async_copy(
                        weight_in.at[pl.ds(found * run + part * chunk, chunk)],
                        weight.at[pl.ds(place * run + part * chunk, chunk)],
                        weight_sem.at[place * chunks + part],
                    )
                )
                copies[-1].start()
        total[...] = jnp.zeros_like(total)
        for copy in small[1:]:
            copy.wait()
        wide = packed[...].astype(F32)
        for source in range(sources):
            grad[source] = wide[:, source].astype(BF16)
        for place in range(count):
            for part in range(chunks):
                copies[place * chunks + part].wait()
                for slot in range(part * chunk, (part + 1) * chunk):
                    entry = firsts[place] + slot
                    where = jnp.where(entry < live[0], tgt[entry], halves)
                    total[place, where, :channels, :] += jnp.dot(
                        grad[src[entry]], weight[place * run + slot], preferred_element_type=F32
                    )
            sums = total[place, :halves].reshape(blocks, 2, padded, half)
            moved = jnp.dot(
                sums[:, 0].reshape(blocks * padded, half).astype(BF16),
                perm_ref[:half],
                preferred_element_type=F32,
            ) + jnp.dot(
                sums[:, 1].reshape(blocks * padded, half).astype(BF16),
                perm_ref[half:],
                preferred_element_type=F32,
            )
            out_refs[2 * place][...] = moved[:, :half].astype(BF16)
            out_refs[2 * place + 1][...] = moved[:, half:].astype(BF16)

    perm = constant(permutation_matrix())
    out = jax.ShapeDtypeStruct((blocks * padded, half), BF16)
    there = pl.BlockSpec(memory_space=pltpu.HBM)
    anywhere = pl.BlockSpec(memory_space=pl.ANY)
    here = pl.BlockSpec(memory_space=pltpu.VMEM)
    operands = [
        pltpu.with_memory_space_constraint(operand, pltpu.HBM)
        for operand in (
            src_block,
            target_half,
            owner,
            latlon_grad.transpose(1, 0, 2),
            remap_weight,
        )
    ]
    results = pl.pallas_call(
        kernel,
        in_specs=[pl.BlockSpec(memory_space=pltpu.SMEM)] + [there] * 5 + [here] + [anywhere] * len(kept),
        out_specs=[here] * (2 * count) + [anywhere] * len(kept),
        out_shape=[out] * (2 * count)
        + [jax.ShapeDtypeStruct(value.shape, value.dtype) for value in kept],
        input_output_aliases={7 + index: 2 * count + index for index in range(len(kept))},
        scratch_shapes=[
            pltpu.SMEM((slots,), jnp.int32),
            pltpu.SMEM((slots,), jnp.int32),
            pltpu.SMEM((slots,), jnp.int32),
            pltpu.VMEM((channels, sources, half), BF16),
            pltpu.VMEM((sources, channels, half), BF16),
            pltpu.VMEM((count * run, half, half), BF16),
            pltpu.VMEM((count, halves + 1, padded, half), F32),
            pltpu.SemaphoreType.DMA((4,)),
            pltpu.SemaphoreType.DMA((count * chunks,)),
        ],
        compiler_params=pltpu.CompilerParams(vmem_limit_bytes=VMEM_LIMIT),
        name="remap",
    )(live_count, *operands, perm, *kept)
    return results[0 : 2 * count : 2], results[1 : 2 * count : 2], results[2 * count :]


def sum_edges(parts, blocks, padded):
    pairs = (blocks + 1) // 2

    def kernel(*refs):
        part_refs, sum_ref, edge_ref = refs[:-2], refs[-2], refs[-1]
        total = part_refs[0][...].astype(F32)
        for ref in part_refs[1:]:
            total = total + ref[...].astype(F32)
        sum_ref[...] = total.astype(BF16)
        lane = lax.broadcasted_iota(jnp.int32, (padded, LANES), 1)
        packed = []
        for pair in range(pairs):
            left = total[2 * pair * padded : (2 * pair + 1) * padded]
            if 2 * pair + 1 < blocks:
                right = total[(2 * pair + 1) * padded : (2 * pair + 2) * padded]
                right = pltpu.roll(right, LANES // 2, 1)
            else:
                right = jnp.zeros_like(left)
            packed.append(jnp.where(lane < LANES // 2, left, right))
        edge_ref[...] = jnp.concatenate(packed, axis=0).astype(BF16)

    return pl.pallas_call(
        kernel,
        out_shape=[
            jax.ShapeDtypeStruct((blocks * padded, LANES), BF16),
            jax.ShapeDtypeStruct((pairs * padded, LANES), BF16),
        ],
        compiler_params=pltpu.CompilerParams(vmem_limit_bytes=VMEM_LIMIT),
        name="sum_edges",
    )(*parts)


def prepare(conv_weight, nbr_block, nbr_code, padded, after):
    taps, channels, hidden = conv_weight.shape
    blocks = nbr_block.shape[0]
    pairs = (blocks + 1) // 2
    devices = lax.axis_size(("tile", "chan"))
    columns = 3 * pairs * LANES
    slots = blocks * 4 * SIDE

    def kernel(nbr, code, taps_ref, unread, weight_ref, rim_ref, pick_ref):
        me = lax.axis_index(("tile", "chan"))
        empty = jnp.zeros((padded - channels, hidden), F32)
        rows = []
        for tap in range(taps):
            rows.append(jnp.concatenate([taps_ref[tap].astype(F32), empty], axis=0))
        weight_ref[...] = jnp.concatenate(rows, axis=0).T.astype(BF16)
        for side in range(4):
            chosen = [rows[tap] for tap in rim_taps(side)]
            rim_ref[side * hidden : (side + 1) * hidden] = (
                jnp.concatenate(chosen, axis=0).T.astype(BF16)
            )
        lane = lax.broadcasted_iota(jnp.int32, (1, slots), 1)
        which = lane // SIDE
        position = lane % SIDE
        start = jnp.zeros((1, slots), jnp.int32)
        turned = jnp.zeros((1, slots), jnp.int32)
        for block in range(blocks):
            for side in range(4):
                other = nbr[side, block]
                turn = code[side, block]
                relative = lax.rem(other // blocks - me + 1 + devices, devices)
                column = (relative * 2 * pairs + lax.rem(other, blocks)) * 64 + turn // 2 * SIDE
                start = jnp.where(which == 4 * block + side, column, start)
                turned = jnp.where(which == 4 * block + side, turn % 2, turned)
        source = start + jnp.where(turned == 1, SIDE - 1 - position, position)
        row = lax.broadcasted_iota(jnp.int32, (columns, slots), 0)
        pick_ref[...] = jnp.where(row == source, 1.0, 0.0).astype(BF16)

    smem = pl.BlockSpec(memory_space=pltpu.SMEM)
    vmem = pl.BlockSpec(memory_space=pltpu.VMEM)
    return pl.pallas_call(
        kernel,
        in_specs=[smem, smem, vmem, pl.BlockSpec(memory_space=pl.ANY)],
        out_specs=[vmem] * 3,
        out_shape=[
            jax.ShapeDtypeStruct((hidden, taps * padded), BF16),
            jax.ShapeDtypeStruct((4 * hidden, 3 * padded), BF16),
            jax.ShapeDtypeStruct((columns, slots), BF16),
        ],
        compiler_params=pltpu.CompilerParams(vmem_limit_bytes=VMEM_LIMIT),
        name="prepare",
    )(nbr_block.T, nbr_code.T, conv_weight, after)


def incoming_rims(edges, rim_weight, pick, blocks, padded):
    pairs = (blocks + 1) // 2
    hidden = rim_weight.shape[0] // 4
    groups = 3 * pairs
    slots = pick.shape[1]

    def kernel(before_ref, own_ref, after_ref, weight_ref, pick_ref, edge_ref, out_ref):
        sides = lax.broadcasted_iota(jnp.int32, (hidden, 2 * LANES), 1) // SIDE % 4
        stacks = []
        for ref in (before_ref, own_ref, after_ref):
            shifted = jnp.dot(ref[...], edge_ref[...], preferred_element_type=F32)
            for pair in range(pairs):
                rows = shifted[pair * padded : (pair + 1) * padded]
                stacks.append(
                    jnp.concatenate([rows[:, LANES * d : LANES * (d + 1)] for d in range(3)], axis=0)
                )
        total = jnp.zeros((hidden, slots), F32)
        for group in range(0, groups, 2):
            stack = jnp.concatenate(stacks[group : group + 2], axis=1).astype(BF16)
            width = stack.shape[1]
            every = jnp.dot(weight_ref[...], stack, preferred_element_type=F32)
            rims = every[:hidden]
            for side in range(1, 4):
                rims = jnp.where(
                    sides[:, :width] == side, every[side * hidden : (side + 1) * hidden], rims
                )
            total = total + jnp.dot(
                rims.astype(BF16),
                pick_ref[group * LANES : group * LANES + width],
                preferred_element_type=F32,
            )
        out_ref[...] = total.astype(BF16)

    return pl.pallas_call(
        kernel,
        out_shape=jax.ShapeDtypeStruct((hidden, slots), BF16),
        compiler_params=pltpu.CompilerParams(vmem_limit_bytes=VMEM_LIMIT),
        name="rims",
    )(*edges, rim_weight, pick, constant(edge_matrix()))


def convolve(first, second_parts, weight, incoming, blocks, padded):
    hidden = weight.shape[0]
    parts = len(second_parts)

    def kernel(*refs):
        first_ref, part_refs = refs[0], refs[1 : 1 + parts]
        weight_ref, incoming_ref, shift_ref, place_ref = refs[1 + parts : 5 + parts]
        out_ref, stack = refs[5 + parts :]
        total = part_refs[0][...].astype(F32)
        for ref in part_refs[1:]:
            total = total + ref[...].astype(F32)
        second = total.astype(BF16)
        for tap in range(TAPS):
            moved = jnp.dot(
                first_ref[...], shift_ref[tap, :LANES], preferred_element_type=F32
            ) + jnp.dot(second, shift_ref[tap, LANES:], preferred_element_type=F32)
            stack[:, padded * tap : padded * (tap + 1), :] = moved.reshape(blocks, padded, CELLS)
        for block in range(blocks):
            grad = jnp.dot(
                weight_ref[...], stack[block].astype(BF16), preferred_element_type=F32
            ) + jnp.dot(
                incoming_ref[:, 64 * block : 64 * (block + 1)],
                place_ref[...],
                preferred_element_type=F32,
            )
            out_ref[block] = grad.astype(BF16)

    return pl.pallas_call(
        kernel,
        out_shape=jax.ShapeDtypeStruct((blocks, hidden, CELLS), BF16),
        scratch_shapes=[pltpu.VMEM((blocks, TAPS * padded, CELLS), F32)],
        compiler_params=pltpu.CompilerParams(vmem_limit_bytes=VMEM_LIMIT),
        name="convolve",
    )(
        first,
        *second_parts,
        weight,
        incoming,
        constant(shift_matrices()),
        constant(place_matrix()),
    )


def from_behind(value, axis, steps):
    count = lax.axis_size(axis)
    pairs = [(source, (source + steps) % count) for source in range(count)]
    return lax.ppermute(value, axis, pairs)


def summed_here(
    latlon_grad, remap_weight, src_block, owner, target_half, live_count, blocks, padded
):
    tiles = lax.axis_size("tile")
    operands = (
        latlon_grad, remap_weight, src_block, owner, target_half, live_count, blocks, padded
    )
    lead = tiles // 2
    shifts = [shift for shift in range(1, tiles) if shift != lead] + [0]
    (first,), (second,), _ = remap_runs([lead], *operands, ())
    first_parts = [from_behind(first, "tile", lead)]
    firsts, seconds, (second,) = remap_runs(shifts, *operands, (second,))
    first_parts += [from_behind(part, "tile", shift) for part, shift in zip(firsts, shifts) if shift]
    second_parts = [from_behind(second, "tile", lead)]
    second_parts += [from_behind(part, "tile", shift) for part, shift in zip(seconds, shifts) if shift]
    return first_parts + [firsts[-1]], second_parts + [seconds[-1]]


def summed_there(
    latlon_grad, remap_weight, src_block, owner, target_half, live_count, blocks, padded
):
    slots, half = remap_weight.shape[:2]
    channels = latlon_grad.shape[1]
    tiles = lax.axis_size("tile")
    run = slots // tiles
    live = jnp.arange(slots, dtype=jnp.int32) < live_count[0]
    runs = jnp.argsort(owner.reshape(tiles, run)[:, 0])
    picked = jnp.take(latlon_grad, src_block, axis=0)
    product = jnp.einsum("eoa,eab->eob", picked, remap_weight, preferred_element_type=F32)
    product = jnp.where(live[:, None, None], product, 0).astype(BF16)
    outgoing = jnp.take(product.reshape(tiles, run, channels, half), runs, axis=0)
    ids = jnp.take(target_half.reshape(tiles, run), runs, axis=0)
    arrived = lax.all_to_all(outgoing, "tile", split_axis=0, concat_axis=0, tiled=True)
    ids = lax.all_to_all(ids, "tile", split_axis=0, concat_axis=0, tiled=True).reshape(slots)
    selector = (jnp.arange(2 * blocks, dtype=jnp.int32)[:, None] == ids[None, :]).astype(BF16)
    sums = jnp.einsum(
        "hs,soa->hoa",
        selector,
        arrived.reshape(slots, channels, half),
        preferred_element_type=F32,
    ).astype(BF16)
    cells = sums.reshape(blocks, 2, channels, half).transpose(0, 2, 1, 3)
    cells = cells.reshape(blocks, channels, 2 * half)[:, :, np.array(lane_order())]
    cells = jnp.pad(cells, ((0, 0), (0, padded - channels), (0, 0)))
    cells = cells.reshape(blocks * padded, 2 * half)
    return [cells[:, :half]], [cells[:, half:]]


def per_device(
    latlon_grad,
    remap_weight,
    src_block,
    owner,
    target_half,
    live_count,
    conv_weight,
    nbr_block,
    nbr_code,
):
    channels = latlon_grad.shape[1]
    hidden = conv_weight.shape[2]
    blocks = nbr_block.shape[0]
    padded = 8 * ((channels + 7) // 8)
    run = remap_weight.shape[0] // lax.axis_size("tile")
    gather = summed_here if run >= 2 * blocks else summed_there
    first_parts, second_parts = gather(
        latlon_grad, remap_weight, src_block, owner, target_half, live_count, blocks, padded
    )
    weight, rim_weight, pick = prepare(conv_weight, nbr_block, nbr_code, padded, first_parts[-1])
    first, edges = sum_edges(first_parts, blocks, padded)
    before = from_behind(edges, ("tile", "chan"), 1)
    after = from_behind(edges, ("tile", "chan"), -1)
    incoming = incoming_rims((before, edges, after), rim_weight, pick, blocks, padded)
    grads = convolve(first, second_parts, weight, incoming, blocks, padded)
    return grads.transpose(1, 0, 2)


def solution(mesh):
    in_specs = (
        P(("member", "tile", "chan"), None, None),
        P(("tile", "chan"), None, None),
        P(("tile", "chan")),
        P(("tile", "chan")),
        P(("tile", "chan")),
        P(("tile", "chan")),
        P(),
        P(("tile", "chan"), None),
        P(("tile", "chan"), None),
    )
    out_specs = P(None, ("member", "tile", "chan"), None)
    return jax.shard_map(
        per_device, mesh=mesh, in_specs=in_specs, out_specs=out_specs, check_vma=False
    )
```

```python
import functools

import jax
import jax.numpy as jnp
import numpy as np
from jax import lax
from jax.experimental import pallas as pl
from jax.experimental.pallas import tpu as pltpu
from jax.sharding import PartitionSpec as P

BF16 = jnp.bfloat16
F32 = jnp.float32
SIDE = 16
CELLS = SIDE * SIDE
LANES = 128
TAPS = 9
VMEM_LIMIT = 48 * 1024 * 1024
PIECES = 3


def edge_cell(side, position):
    return (
        position,
        SIDE * position,
        SIDE * (SIDE - 1) + position,
        SIDE * position + SIDE - 1,
    )[side]


def lane_order():
    edges = sorted({edge_cell(side, position) for side in range(4) for position in range(SIDE)})
    inner = [cell for cell in range(CELLS) if cell not in set(edges)]
    return edges + inner


def permutation_matrix():
    order = lane_order()
    matrix = np.zeros((CELLS, CELLS), np.float32)
    for lane, cell in enumerate(order):
        matrix[cell, lane] = 1
    return matrix


def shift_matrices():
    order = lane_order()
    matrix = np.zeros((TAPS, CELLS, CELLS), np.float32)
    for tap in range(TAPS):
        down, right = tap // 3 - 1, tap % 3 - 1
        for lane, cell in enumerate(order):
            row, column = cell // SIDE + down, cell % SIDE + right
            if 0 <= row < SIDE and 0 <= column < SIDE:
                matrix[tap, lane, row * SIDE + column] = 1
    return matrix


def edge_matrix(pairs):
    lane_of = {cell: lane for lane, cell in enumerate(lane_order())}
    matrix = np.zeros((pairs, 2, 64, 3, 4, pairs, 2, SIDE), np.float32)
    for shift in (-1, 0, 1):
        for side in range(4):
            for position in range(SIDE):
                if 0 <= position - shift < SIDE:
                    lane = lane_of[edge_cell(side, position - shift)]
                    for pair in range(pairs):
                        for half in range(2):
                            matrix[pair, half, lane, shift + 1, side, pair, half, position] = 1
    return matrix.reshape(pairs * LANES, 12 * 2 * SIDE * pairs)


def place_matrix():
    matrix = np.zeros((4, SIDE, CELLS), np.float32)
    for side in range(4):
        for position in range(SIDE):
            matrix[side, position, edge_cell(side, position)] = 1
    return matrix.reshape(4 * SIDE, CELLS)


def rim_taps(side):
    return [((0 + d), 3 * d, 6 + d, 3 * d + 2)[side] for d in range(3)]


def pack_matrices():
    even = permutation_matrix()
    odd = np.concatenate([even[:, 64:128], even[:, :64], even[:, 128:]], axis=1)
    return np.stack([even, odd])


def constant(matrix):
    return jnp.asarray(matrix, BF16)


def whole(array):
    rank = array.ndim
    return pl.BlockSpec(array.shape, lambda *_: (0,) * rank)


def piece_rows(blocks, padded):
    tiles = 2 * blocks
    cuts = [-(-tiles * index // PIECES) for index in range(PIECES + 1)]
    cuts[1] = max(cuts[1], (blocks + 1) // 2)
    return [(first * padded, last * padded) for first, last in zip(cuts[:-1], cuts[1:])]


def remap_runs(
    flips,
    kind,
    latlon_grad,
    remap_weight,
    src_block,
    owner,
    target_half,
    live_count,
    blocks,
    padded,
    after=(),
):
    slots, half = remap_weight.shape[:2]
    channels = latlon_grad.shape[1]
    sources = latlon_grad.shape[0]
    tiles = lax.axis_size("tile")
    run = slots // tiles
    count = len(flips)
    halves = 2 * blocks
    odds = blocks // 2
    pieces = piece_rows(blocks, padded)
    cuts = [0, run // 2] + [run * (index + 1) for index in range(count)]

    def kernel(*refs):
        live, src_in, tgt_in, own_in, grad_in, weight_in, pack_in = refs[:7]
        refs = refs[7 + len(after) :]
        out_refs, refs = refs[: len(pieces)], refs[len(pieces) :]
        src, tgt, own, packed, grad, weight, pack, total, small_sem, weight_sem = refs
        tile = lax.axis_index("tile")
        small = [
            pltpu.make_async_copy(source, target, small_sem.at[index])
            for index, (source, target) in enumerate(
                (
                    (own_in, own),
                    (src_in, src),
                    (tgt_in, tgt),
                    (grad_in, packed),
                    (pack_in, pack),
                )
            )
        ]
        for copy in small[:4]:
            copy.start()
        small[0].wait()
        firsts = []
        for flip in flips:
            wanted = lax.bitwise_xor(tile, flip)
            found = jnp.int32(0)
            for index in range(tiles):
                found = found + jnp.where(own[index * run] == wanted, index, 0)
            firsts.append(found * run)
        large = []
        for part, (start, stop) in enumerate(zip(cuts[:-1], cuts[1:])):
            first = firsts[start // run] + start % run
            large.append(
                pltpu.make_async_copy(
                    weight_in.at[pl.ds(first, stop - start)],
                    weight.at[pl.ds(start, stop - start)],
                    weight_sem.at[part],
                )
            )
            large[-1].start()
        small[4].start()
        total[...] = jnp.zeros_like(total)
        for copy in small[1:4]:
            copy.wait()
        wide = packed[...].astype(F32)
        for source in range(sources):
            grad[source] = wide[:, source].astype(BF16)
        lane = lax.broadcasted_iota(jnp.int32, (odds * padded, half), 1)
        for part, (start, stop) in enumerate(zip(cuts[:-1], cuts[1:])):
            large[part].wait()
            index = start // run
            for slot in range(start, stop):
                entry = firsts[index] + slot % run
                where = jnp.where(entry < live[0], tgt[entry], halves)
                total[index, where, :channels, :] += jnp.dot(
                    grad[src[entry]], weight[slot], preferred_element_type=F32
                )
            if stop % run:
                continue
            if index == 0:
                small[4].wait()
            moved = []
            for parity in range(2):
                joined = jnp.concatenate(
                    [
                        jnp.concatenate(
                            [total[index, 2 * block], total[index, 2 * block + 1]], axis=1
                        )
                        for block in range(parity, blocks, 2)
                    ],
                    axis=0,
                )
                moved.append(
                    jnp.dot(joined.astype(BF16), pack[parity], preferred_element_type=F32)
                )
            both = odds * padded
            edges = jnp.where(lane < 64, moved[0][:both, :half], moved[1][:, :half])
            middle = jnp.where(lane < 64, moved[1][:, :half], moved[0][:both, :half])
            rows = jnp.concatenate(
                [
                    edges,
                    moved[0][both:, :half],
                    middle,
                    moved[0][:, half:],
                    moved[1][:, half:],
                ],
                axis=0,
            )
            for ref, (first, last) in zip(out_refs, pieces):
                size = last - first
                ref[size * index : size * (index + 1)] = rows[first:last].astype(kind)

    operands = [
        pltpu.with_memory_space_constraint(operand, pltpu.HBM)
        for operand in (
            src_block,
            target_half,
            owner,
            latlon_grad.transpose(1, 0, 2),
            remap_weight,
            constant(pack_matrices()),
        )
    ]
    return pl.pallas_call(
        kernel,
        in_specs=[pl.BlockSpec(memory_space=pltpu.SMEM)]
        + [pl.BlockSpec(memory_space=pltpu.HBM)] * 6
        + [pl.BlockSpec(memory_space=pl.ANY)] * len(after),
        out_specs=[pl.BlockSpec(memory_space=pltpu.VMEM)] * len(pieces),
        out_shape=[
            jax.ShapeDtypeStruct((count * (last - first), half), kind) for first, last in pieces
        ],
        scratch_shapes=[
            pltpu.SMEM((slots,), jnp.int32),
            pltpu.SMEM((slots,), jnp.int32),
            pltpu.SMEM((slots,), jnp.int32),
            pltpu.VMEM((channels, sources, half), BF16),
            pltpu.VMEM((sources, channels, half), BF16),
            pltpu.VMEM((count * run, half, half), BF16),
            pltpu.VMEM((2, 2 * half, 2 * half), BF16),
            pltpu.VMEM((count, halves + 1, padded, half), F32),
            pltpu.SemaphoreType.DMA((5,)),
            pltpu.SemaphoreType.DMA((len(cuts) - 1,)),
        ],
        compiler_params=pltpu.CompilerParams(vmem_limit_bytes=VMEM_LIMIT),
        name="remap",
    )(live_count, *operands, *after)


def add_halves(kept, arrived, after=()):
    rows = kept.shape[0] // 2

    def kernel(kept_ref, arrived_ref, *refs):
        here_ref, there_ref = refs[len(after) :]
        here_ref[...] = kept_ref[:rows] + arrived_ref[:rows].astype(F32)
        there_ref[...] = (kept_ref[rows:] + arrived_ref[rows:].astype(F32)).astype(BF16)

    vmem = pl.BlockSpec(memory_space=pltpu.VMEM)
    return pl.pallas_call(
        kernel,
        in_specs=[vmem] * 2 + [pl.BlockSpec(memory_space=pl.ANY)] * len(after),
        out_specs=[vmem] * 2,
        out_shape=[
            jax.ShapeDtypeStruct((rows, kept.shape[1]), F32),
            jax.ShapeDtypeStruct((rows, kept.shape[1]), BF16),
        ],
        compiler_params=pltpu.CompilerParams(vmem_limit_bytes=VMEM_LIMIT),
        name="add_halves",
    )(kept, arrived, *after)


def sum_parts(parts, edge_rows):
    def kernel(*refs):
        total = refs[0][...].astype(F32)
        for ref in refs[1:-2]:
            total = total + ref[...].astype(F32)
        total = total.astype(BF16)
        refs[-2][...] = total
        refs[-1][...] = total[:edge_rows]

    return pl.pallas_call(
        kernel,
        out_shape=[
            jax.ShapeDtypeStruct(parts[0].shape, BF16),
            jax.ShapeDtypeStruct((edge_rows, parts[0].shape[1]), BF16),
        ],
        compiler_params=pltpu.CompilerParams(vmem_limit_bytes=VMEM_LIMIT),
        name="sum_parts",
    )(*parts)


def split_rows(padded):
    full = 16 * (padded // 16)
    return full, 16 * ((TAPS * (padded - full) + 15) // 16)


def prepare(conv_weight, nbr_block, nbr_code, padded, after):
    taps, channels, hidden = conv_weight.shape
    blocks = nbr_block.shape[0]
    pairs = (blocks + 1) // 2
    devices = lax.axis_size(("tile", "chan"))
    span = 2 * SIDE * pairs
    columns = 4 * 3 * span
    slots = blocks * 4 * SIDE
    full, rest = split_rows(padded)

    def kernel(nbr, code, taps_ref, unread, weight_ref, rim_ref, pick_ref):
        me = lax.axis_index(("tile", "chan"))
        empty = jnp.zeros((padded - channels, hidden), F32)
        rows = []
        for tap in range(taps):
            rows.append(jnp.concatenate([taps_ref[tap].astype(F32), empty], axis=0))
        tail = jnp.zeros((rest - taps * (padded - full), hidden), F32)
        stacked = [row[:full] for row in rows] + [row[full:] for row in rows] + [tail]
        weight_ref[...] = jnp.concatenate(stacked, axis=0).T.astype(BF16)
        for side in range(4):
            chosen = [rows[tap] for tap in rim_taps(side)]
            rim_ref[side * hidden : (side + 1) * hidden] = (
                jnp.concatenate(chosen, axis=0).T.astype(BF16)
            )
        lane = lax.broadcasted_iota(jnp.int32, (1, slots), 1)
        which = lane // SIDE
        position = lane % SIDE
        start = jnp.zeros((1, slots), jnp.int32)
        turned = jnp.zeros((1, slots), jnp.int32)
        for block in range(blocks):
            for side in range(4):
                other = nbr[side, block]
                turn = code[side, block]
                relative = lax.rem(other // blocks - me + 1 + devices, devices)
                column = (turn // 2 * 3 + relative) * span + lax.rem(other, blocks) * SIDE
                start = jnp.where(which == 4 * block + side, column, start)
                turned = jnp.where(which == 4 * block + side, turn % 2, turned)
        source = start + jnp.where(turned == 1, SIDE - 1 - position, position)
        row = lax.broadcasted_iota(jnp.int32, (columns, slots), 0)
        pick_ref[...] = jnp.where(row == source, 1.0, 0.0).astype(BF16)

    smem = pl.BlockSpec(memory_space=pltpu.SMEM)
    vmem = pl.BlockSpec(memory_space=pltpu.VMEM)
    return pl.pallas_call(
        kernel,
        in_specs=[smem, smem, vmem, pl.BlockSpec(memory_space=pl.ANY)],
        out_specs=[vmem] * 3,
        out_shape=[
            jax.ShapeDtypeStruct((hidden, taps * full + rest), BF16),
            jax.ShapeDtypeStruct((4 * hidden, 3 * padded), BF16),
            jax.ShapeDtypeStruct((columns, slots), BF16),
        ],
        compiler_params=pltpu.CompilerParams(vmem_limit_bytes=VMEM_LIMIT),
        name="prepare",
    )(nbr_block.T, nbr_code.T, conv_weight, after)


def incoming_rims(edges, rim_weight, pick, blocks, padded):
    pairs = (blocks + 1) // 2
    span = 2 * SIDE * pairs
    hidden = rim_weight.shape[0] // 4
    slots = pick.shape[1]

    def kernel(before_ref, own_ref, after_ref, weight_ref, pick_ref, edge_ref, out_ref):
        rows = []
        for ref in (before_ref, own_ref, after_ref):
            edges = ref[...].astype(F32)
            rows.append(
                jnp.concatenate(
                    [edges[pair * padded : (pair + 1) * padded] for pair in range(pairs)], axis=1
                )
            )
        shifted = jnp.dot(
            jnp.concatenate(rows, axis=0).astype(BF16),
            edge_ref[...],
            preferred_element_type=F32,
        )
        total = jnp.zeros((hidden, slots), F32)
        for side in range(4):
            stack = jnp.concatenate(
                [
                    jnp.concatenate(
                        [
                            shifted[
                                device * padded : (device + 1) * padded,
                                (4 * shift + side) * span : (4 * shift + side + 1) * span,
                            ]
                            for device in range(3)
                        ],
                        axis=1,
                    )
                    for shift in range(3)
                ],
                axis=0,
            ).astype(BF16)
            rims = jnp.dot(
                weight_ref[side * hidden : (side + 1) * hidden],
                stack,
                preferred_element_type=F32,
            ).astype(BF16)
            total = total + jnp.dot(
                rims,
                pick_ref[side * 3 * span : (side + 1) * 3 * span],
                preferred_element_type=F32,
            )
        out_ref[...] = total.astype(BF16)

    return pl.pallas_call(
        kernel,
        out_shape=jax.ShapeDtypeStruct((hidden, slots), BF16),
        compiler_params=pltpu.CompilerParams(vmem_limit_bytes=VMEM_LIMIT),
        name="rims",
    )(*edges, rim_weight, pick, constant(edge_matrix(pairs)))


def convolve(pieces, weight, incoming, blocks, padded):
    hidden = weight.shape[0]
    flat = [part for piece in pieces for part in piece]
    parts = len(flat)
    full, rest = split_rows(padded)
    evens, odds = (blocks + 1) // 2, blocks // 2
    order = [*range(0, blocks, 2), *range(1, blocks, 2)]

    def kernel(*refs):
        part_refs = list(refs[:parts])
        weight_ref, incoming_ref, shift_ref, place_ref = refs[parts : 4 + parts]
        out_ref, stack, result, sems = refs[4 + parts :]
        copies = []
        totals = []
        for piece in pieces:
            total = part_refs.pop(0)[...].astype(F32)
            for _ in piece[1:]:
                total = total + part_refs.pop(0)[...].astype(F32)
            totals.append(total)
        total = jnp.concatenate(totals, axis=0)
        edge_rows, both = evens * padded, odds * padded
        edge, middle = total[:both], total[edge_rows : edge_rows + both]
        lane = lax.broadcasted_iota(jnp.int32, (both, LANES), 1)
        even = jnp.where(lane < 64, edge, middle)
        odd = pltpu.roll(jnp.where(lane < 64, middle, edge), 64, 1)
        lead = jnp.concatenate([even, total[both:edge_rows], odd], axis=0)
        cells = jnp.concatenate([lead, total[edge_rows + both :]], axis=1).astype(BF16)
        rests = []
        for tap in range(TAPS):
            moved = jnp.dot(cells, shift_ref[tap], preferred_element_type=F32)
            moved = moved.reshape(blocks, padded, CELLS)
            stack[:, full * tap : full * (tap + 1), :] = moved[:, :full].astype(BF16)
            rests.append(moved[:, full:])
        rests.append(jnp.zeros((blocks, rest - TAPS * (padded - full), CELLS), F32))
        stack[:, full * TAPS :, :] = jnp.concatenate(rests, axis=1).astype(BF16)
        for index, block in enumerate(order):
            grad = jnp.dot(
                weight_ref[...], stack[index], preferred_element_type=F32
            ) + jnp.dot(
                incoming_ref[:, 64 * block : 64 * (block + 1)],
                place_ref[...],
                preferred_element_type=F32,
            )
            result[block] = grad.astype(BF16)
            copies.append(
                pltpu.make_async_copy(result.at[block], out_ref.at[block], sems.at[block])
            )
            copies[-1].start()
        for copy in copies:
            copy.wait()

    return pl.pallas_call(
        kernel,
        out_shape=jax.ShapeDtypeStruct((blocks, hidden, CELLS), BF16),
        out_specs=pl.BlockSpec(memory_space=pltpu.HBM),
        scratch_shapes=[
            pltpu.VMEM((blocks, TAPS * full + rest, CELLS), BF16),
            pltpu.VMEM((blocks, hidden, CELLS), BF16),
            pltpu.SemaphoreType.DMA((blocks,)),
        ],
        compiler_params=pltpu.CompilerParams(vmem_limit_bytes=VMEM_LIMIT),
        name="convolve",
    )(
        *flat,
        weight,
        incoming,
        constant(shift_matrices()),
        constant(place_matrix()),
    )


def from_behind(value, axis, steps):
    count = lax.axis_size(axis)
    pairs = [(source, (source + steps) % count) for source in range(count)]
    return lax.ppermute(value, axis, pairs)


def swapped(value, flip):
    pairs = [(source, source ^ flip) for source in range(lax.axis_size("tile"))]
    return lax.ppermute(value, "tile", pairs)


def summed_here(
    prepare, latlon_grad, remap_weight, src_block, owner, target_half, live_count, blocks, padded
):
    operands = (
        latlon_grad, remap_weight, src_block, owner, target_half, live_count, blocks, padded
    )
    moving = list(remap_runs((1, 3), BF16, *operands))
    kept = remap_runs((0, 2), F32, *operands, (moving[0],))
    ready = prepare(kept[0])
    pieces = []
    for index, stays in enumerate(kept):
        arrives = swapped(moving[index], 1)
        stays, leaves = add_halves(stays, arrives, ())
        pieces.append([stays, swapped(leaves, 2)])
    return pieces, ready


def summed_there(
    prepare, latlon_grad, remap_weight, src_block, owner, target_half, live_count, blocks, padded
):
    slots, half = remap_weight.shape[:2]
    channels = latlon_grad.shape[1]
    tiles = lax.axis_size("tile")
    run = slots // tiles
    live = jnp.arange(slots, dtype=jnp.int32) < live_count[0]
    runs = jnp.argsort(owner.reshape(tiles, run)[:, 0])
    picked = jnp.take(latlon_grad, src_block, axis=0)
    product = jnp.einsum("eoa,eab->eob", picked, remap_weight, preferred_element_type=F32)
    product = jnp.where(live[:, None, None], product, 0).astype(BF16)
    outgoing = jnp.take(product.reshape(tiles, run, channels, half), runs, axis=0)
    ids = jnp.take(target_half.reshape(tiles, run), runs, axis=0)
    arrived = lax.all_to_all(outgoing, "tile", split_axis=0, concat_axis=0, tiled=True)
    ids = lax.all_to_all(ids, "tile", split_axis=0, concat_axis=0, tiled=True).reshape(slots)
    selector = (jnp.arange(2 * blocks, dtype=jnp.int32)[:, None] == ids[None, :]).astype(BF16)
    sums = jnp.einsum(
        "hs,soa->hoa",
        selector,
        arrived.reshape(slots, channels, half),
        preferred_element_type=F32,
    ).astype(BF16)
    cells = sums.reshape(blocks, 2, channels, half).transpose(0, 2, 1, 3)
    cells = cells.reshape(blocks, channels, 2 * half)[:, :, np.array(lane_order())]
    cells = jnp.pad(cells, ((0, 0), (0, padded - channels), (0, 0)))
    even, odd = cells[0::2], cells[1::2]
    count = blocks // 2
    edges = jnp.concatenate([even[:count, :, :64], odd[:, :, :64]], axis=2)
    middle = jnp.concatenate([odd[:, :, 64:128], even[:count, :, 64:128]], axis=2)
    rows = jnp.concatenate(
        [edges, even[count:, :, :128], middle, even[:, :, 128:], odd[:, :, 128:]], axis=0
    )
    rows = rows.reshape(-1, half)
    pieces = [[rows[first:last]] for first, last in piece_rows(blocks, padded)]
    return pieces, prepare(rows)


def per_device(
    latlon_grad,
    remap_weight,
    src_block,
    owner,
    target_half,
    live_count,
    conv_weight,
    nbr_block,
    nbr_code,
):
    channels = latlon_grad.shape[1]
    hidden = conv_weight.shape[2]
    blocks = nbr_block.shape[0]
    padded = 8 * ((channels + 7) // 8)
    run = remap_weight.shape[0] // lax.axis_size("tile")
    small = lax.axis_size("tile") == 4 and run >= 2 * blocks
    gather = summed_here if small else summed_there
    ready = functools.partial(prepare, conv_weight, nbr_block, nbr_code, padded)
    pieces, (weight, rim_weight, pick) = gather(
        ready,
        latlon_grad,
        remap_weight,
        src_block,
        owner,
        target_half,
        live_count,
        blocks,
        padded,
    )
    lead, edges = sum_parts(pieces[0], (blocks + 1) // 2 * padded)
    pieces[0] = [lead]
    before = from_behind(edges, ("tile", "chan"), 1)
    after = from_behind(edges, ("tile", "chan"), -1)
    incoming = incoming_rims((before, edges, after), rim_weight, pick, blocks, padded)
    grads = convolve(pieces, weight, incoming, blocks, padded)
    return grads.transpose(1, 0, 2)


def solution(mesh):
    in_specs = (
        P(("member", "tile", "chan"), None, None),
        P(("tile", "chan"), None, None),
        P(("tile", "chan")),
        P(("tile", "chan")),
        P(("tile", "chan")),
        P(("tile", "chan")),
        P(),
        P(("tile", "chan"), None),
        P(("tile", "chan"), None),
    )
    out_specs = P(None, ("member", "tile", "chan"), None)
    return jax.shard_map(
        per_device, mesh=mesh, in_specs=in_specs, out_specs=out_specs, check_vma=False
    )
```

```python
import functools

import jax
import jax.numpy as jnp
import numpy as np
from jax import lax
from jax.experimental import pallas as pl
from jax.experimental.pallas import tpu as pltpu
from jax.sharding import PartitionSpec as P

BF16 = jnp.bfloat16
F32 = jnp.float32
SIDE = 16
CELLS = SIDE * SIDE
LANES = 128
TAPS = 9
VMEM_LIMIT = 48 * 1024 * 1024
SHARES = (6, 5, 3)


def edge_cell(side, position):
    return (
        position,
        SIDE * position,
        SIDE * (SIDE - 1) + position,
        SIDE * position + SIDE - 1,
    )[side]


def lane_order():
    edges = sorted({edge_cell(side, position) for side in range(4) for position in range(SIDE)})
    inner = [cell for cell in range(CELLS) if cell not in set(edges)]
    return edges + inner


def permutation_matrix():
    order = lane_order()
    matrix = np.zeros((CELLS, CELLS), np.float32)
    for lane, cell in enumerate(order):
        matrix[cell, lane] = 1
    return matrix


def shift_matrices():
    order = lane_order()
    matrix = np.zeros((TAPS, CELLS, CELLS), np.float32)
    for tap in range(TAPS):
        down, right = tap // 3 - 1, tap % 3 - 1
        for lane, cell in enumerate(order):
            row, column = cell // SIDE + down, cell % SIDE + right
            if 0 <= row < SIDE and 0 <= column < SIDE:
                matrix[tap, lane, row * SIDE + column] = 1
    return matrix


def edge_matrix(pairs):
    lane_of = {cell: lane for lane, cell in enumerate(lane_order())}
    matrix = np.zeros((pairs, 2, 64, 3, 4, pairs, 2, SIDE), np.float32)
    for shift in (-1, 0, 1):
        for side in range(4):
            for position in range(SIDE):
                if 0 <= position - shift < SIDE:
                    lane = lane_of[edge_cell(side, position - shift)]
                    for pair in range(pairs):
                        for half in range(2):
                            matrix[pair, half, lane, shift + 1, side, pair, half, position] = 1
    return matrix.reshape(pairs * LANES, 12 * 2 * SIDE * pairs)


def place_matrix():
    matrix = np.zeros((4, SIDE, CELLS), np.float32)
    for side in range(4):
        for position in range(SIDE):
            matrix[side, position, edge_cell(side, position)] = 1
    return matrix.reshape(4 * SIDE, CELLS)


def rim_taps(side):
    return [((0 + d), 3 * d, 6 + d, 3 * d + 2)[side] for d in range(3)]


def pack_matrices():
    even = permutation_matrix()
    odd = np.concatenate([even[:, 64:128], even[:, :64], even[:, 128:]], axis=1)
    return np.stack([even, odd])


def constant(matrix):
    return jnp.asarray(matrix, BF16)


def whole(array):
    rank = array.ndim
    return pl.BlockSpec(array.shape, lambda *_: (0,) * rank)


def piece_rows(blocks, padded):
    tiles = 2 * blocks
    shares = [sum(SHARES[:index]) for index in range(len(SHARES) + 1)]
    cuts = [-(-tiles * share // shares[-1]) for share in shares]
    cuts[1] = max(cuts[1], (blocks + 1) // 2)
    return [(first * padded, last * padded) for first, last in zip(cuts[:-1], cuts[1:])]


def remap_runs(
    flips,
    kind,
    latlon_grad,
    remap_weight,
    src_block,
    owner,
    target_half,
    live_count,
    blocks,
    padded,
    after=(),
):
    slots, half = remap_weight.shape[:2]
    channels = latlon_grad.shape[1]
    sources = latlon_grad.shape[0]
    tiles = lax.axis_size("tile")
    run = slots // tiles
    count = len(flips)
    halves = 2 * blocks
    odds = blocks // 2
    pieces = piece_rows(blocks, padded)
    cuts = [0, run // 2] + [run * (index + 1) for index in range(count)]

    def kernel(*refs):
        live, src_in, tgt_in, own_in, grad_in, weight_in, pack_in = refs[:7]
        refs = refs[7 + len(after) :]
        out_refs, refs = refs[: len(pieces)], refs[len(pieces) :]
        src, tgt, own, packed, grad, weight, pack, total, small_sem, weight_sem = refs
        tile = lax.axis_index("tile")
        small = [
            pltpu.make_async_copy(source, target, small_sem.at[index])
            for index, (source, target) in enumerate(
                (
                    (own_in, own),
                    (src_in, src),
                    (tgt_in, tgt),
                    (grad_in, packed),
                    (pack_in, pack),
                )
            )
        ]
        for copy in small[:4]:
            copy.start()
        small[0].wait()
        firsts = []
        for flip in flips:
            wanted = lax.bitwise_xor(tile, flip)
            found = jnp.int32(0)
            for index in range(tiles):
                found = found + jnp.where(own[index * run] == wanted, index, 0)
            firsts.append(found * run)
        large = []
        for part, (start, stop) in enumerate(zip(cuts[:-1], cuts[1:])):
            first = firsts[start // run] + start % run
            large.append(
                pltpu.make_async_copy(
                    weight_in.at[pl.ds(first, stop - start)],
                    weight.at[pl.ds(start, stop - start)],
                    weight_sem.at[part],
                )
            )
            large[-1].start()
        small[4].start()
        total[...] = jnp.zeros_like(total)
        for copy in small[1:4]:
            copy.wait()
        wide = packed[...].astype(F32)
        for source in range(sources):
            grad[source] = wide[:, source].astype(BF16)
        lane = lax.broadcasted_iota(jnp.int32, (odds * padded, half), 1)
        for part, (start, stop) in enumerate(zip(cuts[:-1], cuts[1:])):
            if part == 0 or start % run:
                large[part].wait()
            index = start // run
            for slot in range(start, stop):
                entry = firsts[index] + slot % run
                where = jnp.where(entry < live[0], tgt[entry], halves)
                total[index, where, :channels, :] += jnp.dot(
                    grad[src[entry]], weight[slot], preferred_element_type=F32
                )
            if stop % run:
                continue
            if index == 0:
                small[4].wait()
            if index + 1 < count:
                large[part + 1].wait()
            moved = []
            for parity in range(2):
                joined = jnp.concatenate(
                    [
                        jnp.concatenate(
                            [total[index, 2 * block], total[index, 2 * block + 1]], axis=1
                        )
                        for block in range(parity, blocks, 2)
                    ],
                    axis=0,
                )
                moved.append(
                    jnp.dot(joined.astype(BF16), pack[parity], preferred_element_type=F32)
                )
            both = odds * padded
            edges = jnp.where(lane < 64, moved[0][:both, :half], moved[1][:, :half])
            middle = jnp.where(lane < 64, moved[1][:, :half], moved[0][:both, :half])
            rows = jnp.concatenate(
                [
                    edges,
                    moved[0][both:, :half],
                    middle,
                    moved[0][:, half:],
                    moved[1][:, half:],
                ],
                axis=0,
            )
            for ref, (first, last) in zip(out_refs, pieces):
                size = last - first
                ref[size * index : size * (index + 1)] = rows[first:last].astype(kind)

    operands = [
        pltpu.with_memory_space_constraint(operand, pltpu.HBM)
        for operand in (
            src_block,
            target_half,
            owner,
            latlon_grad.transpose(1, 0, 2),
            remap_weight,
            constant(pack_matrices()),
        )
    ]
    return pl.pallas_call(
        kernel,
        in_specs=[pl.BlockSpec(memory_space=pltpu.SMEM)]
        + [pl.BlockSpec(memory_space=pltpu.HBM)] * 6
        + [pl.BlockSpec(memory_space=pl.ANY)] * len(after),
        out_specs=[pl.BlockSpec(memory_space=pltpu.VMEM)] * len(pieces),
        out_shape=[
            jax.ShapeDtypeStruct((count * (last - first), half), kind) for first, last in pieces
        ],
        scratch_shapes=[
            pltpu.SMEM((slots,), jnp.int32),
            pltpu.SMEM((slots,), jnp.int32),
            pltpu.SMEM((slots,), jnp.int32),
            pltpu.VMEM((channels, sources, half), BF16),
            pltpu.VMEM((sources, channels, half), BF16),
            pltpu.VMEM((count * run, half, half), BF16),
            pltpu.VMEM((2, 2 * half, 2 * half), BF16),
            pltpu.VMEM((count, halves + 1, padded, half), F32),
            pltpu.SemaphoreType.DMA((5,)),
            pltpu.SemaphoreType.DMA((len(cuts) - 1,)),
        ],
        compiler_params=pltpu.CompilerParams(vmem_limit_bytes=VMEM_LIMIT),
        name="remap",
    )(live_count, *operands, *after)


def add_halves(kept, arrived, after=()):
    rows = kept.shape[0] // 2

    def kernel(kept_ref, arrived_ref, *refs):
        here_ref, there_ref = refs[len(after) :]
        here_ref[...] = kept_ref[:rows] + arrived_ref[:rows].astype(F32)
        there_ref[...] = (kept_ref[rows:] + arrived_ref[rows:].astype(F32)).astype(BF16)

    vmem = pl.BlockSpec(memory_space=pltpu.VMEM)
    return pl.pallas_call(
        kernel,
        in_specs=[vmem] * 2 + [pl.BlockSpec(memory_space=pl.ANY)] * len(after),
        out_specs=[vmem] * 2,
        out_shape=[
            jax.ShapeDtypeStruct((rows, kept.shape[1]), F32),
            jax.ShapeDtypeStruct((rows, kept.shape[1]), BF16),
        ],
        compiler_params=pltpu.CompilerParams(vmem_limit_bytes=VMEM_LIMIT),
        name="add_halves",
    )(kept, arrived, *after)


def sum_parts(parts, edge_rows):
    def kernel(*refs):
        total = refs[0][...].astype(F32)
        for ref in refs[1:-2]:
            total = total + ref[...].astype(F32)
        total = total.astype(BF16)
        refs[-2][...] = total
        refs[-1][...] = total[:edge_rows]

    return pl.pallas_call(
        kernel,
        out_shape=[
            jax.ShapeDtypeStruct(parts[0].shape, BF16),
            jax.ShapeDtypeStruct((edge_rows, parts[0].shape[1]), BF16),
        ],
        compiler_params=pltpu.CompilerParams(vmem_limit_bytes=VMEM_LIMIT),
        name="sum_parts",
    )(*parts)


def split_rows(padded):
    full = 16 * (padded // 16)
    return full, 16 * ((TAPS * (padded - full) + 15) // 16)


def prepare(conv_weight, nbr_block, nbr_code, padded, after):
    taps, channels, hidden = conv_weight.shape
    blocks = nbr_block.shape[0]
    pairs = (blocks + 1) // 2
    devices = lax.axis_size(("tile", "chan"))
    span = 2 * SIDE * pairs
    columns = 4 * 3 * span
    slots = blocks * 4 * SIDE
    full, rest = split_rows(padded)

    def kernel(nbr, code, taps_ref, unread, weight_ref, rim_ref, pick_ref):
        me = lax.axis_index(("tile", "chan"))
        empty = jnp.zeros((padded - channels, hidden), F32)
        rows = []
        for tap in range(taps):
            rows.append(jnp.concatenate([taps_ref[tap].astype(F32), empty], axis=0))
        tail = jnp.zeros((rest - taps * (padded - full), hidden), F32)
        stacked = [row[:full] for row in rows] + [row[full:] for row in rows] + [tail]
        weight_ref[...] = jnp.concatenate(stacked, axis=0).T.astype(BF16)
        for side in range(4):
            chosen = [rows[tap] for tap in rim_taps(side)]
            rim_ref[side * hidden : (side + 1) * hidden] = (
                jnp.concatenate(chosen, axis=0).T.astype(BF16)
            )
        lane = lax.broadcasted_iota(jnp.int32, (1, slots), 1)
        which = lane // SIDE
        position = lane % SIDE
        start = jnp.zeros((1, slots), jnp.int32)
        turned = jnp.zeros((1, slots), jnp.int32)
        for block in range(blocks):
            for side in range(4):
                other = nbr[side, block]
                turn = code[side, block]
                relative = lax.rem(other // blocks - me + 1 + devices, devices)
                part = relative
                column = (turn // 2 * 3 + part) * span + lax.rem(other, blocks) * SIDE
                start = jnp.where(which == 4 * block + side, column, start)
                turned = jnp.where(which == 4 * block + side, turn % 2, turned)
        source = start + jnp.where(turned == 1, SIDE - 1 - position, position)
        row = lax.broadcasted_iota(jnp.int32, (columns, slots), 0)
        pick_ref[...] = jnp.where(row == source, 1.0, 0.0).astype(BF16)

    smem = pl.BlockSpec(memory_space=pltpu.SMEM)
    vmem = pl.BlockSpec(memory_space=pltpu.VMEM)
    return pl.pallas_call(
        kernel,
        in_specs=[smem, smem, vmem, pl.BlockSpec(memory_space=pl.ANY)],
        out_specs=[vmem] * 3,
        out_shape=[
            jax.ShapeDtypeStruct((hidden, taps * full + rest), BF16),
            jax.ShapeDtypeStruct((4 * hidden, 3 * padded), BF16),
            jax.ShapeDtypeStruct((columns, slots), BF16),
        ],
        compiler_params=pltpu.CompilerParams(vmem_limit_bytes=VMEM_LIMIT),
        name="prepare",
    )(nbr_block.T, nbr_code.T, conv_weight, after)


def incoming_rims(edges, rim_weight, pick, blocks, padded):
    pairs = (blocks + 1) // 2
    span = 2 * SIDE * pairs
    hidden = rim_weight.shape[0] // 4
    slots = pick.shape[1]

    def kernel(near_ref, own_ref, far_ref, weight_ref, pick_ref, edge_ref, out_ref):
        rows = []
        for ref in (near_ref, own_ref, far_ref):
            edges = ref[...].astype(F32)
            rows.append(
                jnp.concatenate(
                    [edges[pair * padded : (pair + 1) * padded] for pair in range(pairs)], axis=1
                )
            )
        shifted = jnp.dot(
            jnp.concatenate(rows, axis=0).astype(BF16),
            edge_ref[...],
            preferred_element_type=F32,
        )
        rims = []
        for side in range(4):
            stack = jnp.concatenate(
                [
                    jnp.concatenate(
                        [
                            shifted[
                                device * padded : (device + 1) * padded,
                                (4 * shift + side) * span : (4 * shift + side + 1) * span,
                            ]
                            for device in range(3)
                        ],
                        axis=1,
                    )
                    for shift in range(3)
                ],
                axis=0,
            ).astype(BF16)
            rims.append(
                jnp.dot(
                    weight_ref[side * hidden : (side + 1) * hidden],
                    stack,
                    preferred_element_type=F32,
                ).astype(BF16)
            )
        out_ref[...] = jnp.dot(
            jnp.concatenate(rims, axis=1), pick_ref[...], preferred_element_type=F32
        ).astype(BF16)

    return pl.pallas_call(
        kernel,
        out_shape=jax.ShapeDtypeStruct((hidden, slots), BF16),
        compiler_params=pltpu.CompilerParams(vmem_limit_bytes=VMEM_LIMIT),
        name="rims",
    )(*edges, rim_weight, pick, constant(edge_matrix(pairs)))


def convolve(pieces, weight, incoming, blocks, padded):
    hidden = weight.shape[0]
    flat = [part for piece in pieces for part in piece]
    parts = len(flat)
    full, rest = split_rows(padded)
    evens, odds = (blocks + 1) // 2, blocks // 2
    order = [*range(0, blocks, 2), *range(1, blocks, 2)]

    def kernel(*refs):
        part_refs = list(refs[:parts])
        weight_ref, incoming_ref, shift_ref, place_ref = refs[parts : 4 + parts]
        out_ref, stack, result, sems = refs[4 + parts :]
        copies = []
        totals = []
        for piece in pieces:
            total = part_refs.pop(0)[...].astype(F32)
            for _ in piece[1:]:
                total = total + part_refs.pop(0)[...].astype(F32)
            totals.append(total)
        total = jnp.concatenate(totals, axis=0)
        edge_rows, both = evens * padded, odds * padded
        edge, middle = total[:both], total[edge_rows : edge_rows + both]
        lane = lax.broadcasted_iota(jnp.int32, (both, LANES), 1)
        even = jnp.where(lane < 64, edge, middle)
        odd = pltpu.roll(jnp.where(lane < 64, middle, edge), 64, 1)
        lead = jnp.concatenate([even, total[both:edge_rows], odd], axis=0)
        cells = jnp.concatenate([lead, total[edge_rows + both :]], axis=1).astype(BF16)
        rests = []
        for tap in range(TAPS):
            moved = jnp.dot(cells, shift_ref[tap], preferred_element_type=F32)
            moved = moved.reshape(blocks, padded, CELLS)
            stack[:, full * tap : full * (tap + 1), :] = moved[:, :full].astype(BF16)
            rests.append(moved[:, full:])
        rests.append(jnp.zeros((blocks, rest - TAPS * (padded - full), CELLS), F32))
        stack[:, full * TAPS :, :] = jnp.concatenate(rests, axis=1).astype(BF16)
        for index, block in enumerate(order):
            grad = jnp.dot(
                weight_ref[...], stack[index], preferred_element_type=F32
            ) + jnp.dot(
                incoming_ref[:, 64 * block : 64 * (block + 1)],
                place_ref[...],
                preferred_element_type=F32,
            )
            result[block] = grad.astype(BF16)
            copies.append(
                pltpu.make_async_copy(result.at[block], out_ref.at[block], sems.at[block])
            )
            copies[-1].start()
        for copy in copies:
            copy.wait()

    return pl.pallas_call(
        kernel,
        out_shape=jax.ShapeDtypeStruct((blocks, hidden, CELLS), BF16),
        out_specs=pl.BlockSpec(memory_space=pltpu.HBM),
        scratch_shapes=[
            pltpu.VMEM((blocks, TAPS * full + rest, CELLS), BF16),
            pltpu.VMEM((blocks, hidden, CELLS), BF16),
            pltpu.SemaphoreType.DMA((blocks,)),
        ],
        compiler_params=pltpu.CompilerParams(vmem_limit_bytes=VMEM_LIMIT),
        name="convolve",
    )(
        *flat,
        weight,
        incoming,
        constant(shift_matrices()),
        constant(place_matrix()),
    )


def swapped(value, flip):
    pairs = [(source, source ^ flip) for source in range(lax.axis_size("tile"))]
    return lax.ppermute(value, "tile", pairs)


def summed_here(
    prepare, latlon_grad, remap_weight, src_block, owner, target_half, live_count, blocks, padded
):
    operands = (
        latlon_grad, remap_weight, src_block, owner, target_half, live_count, blocks, padded
    )
    moving = list(remap_runs((1, 3), BF16, *operands))
    kept = remap_runs((0, 2), F32, *operands, (moving[0],))
    pieces = []
    for index, stays in enumerate(kept):
        stays, leaves = add_halves(stays, swapped(moving[index], 1))
        if index == 0:
            weight, *ready = prepare(leaves)
            weight, moving[-1] = lax.optimization_barrier((weight, moving[-1]))
        pieces.append([stays, swapped(leaves, 2)])
    return pieces, (weight, *ready)


def summed_there(
    prepare, latlon_grad, remap_weight, src_block, owner, target_half, live_count, blocks, padded
):
    slots, half = remap_weight.shape[:2]
    channels = latlon_grad.shape[1]
    tiles = lax.axis_size("tile")
    run = slots // tiles
    live = jnp.arange(slots, dtype=jnp.int32) < live_count[0]
    runs = jnp.argsort(owner.reshape(tiles, run)[:, 0])
    picked = jnp.take(latlon_grad, src_block, axis=0)
    product = jnp.einsum("eoa,eab->eob", picked, remap_weight, preferred_element_type=F32)
    product = jnp.where(live[:, None, None], product, 0).astype(BF16)
    outgoing = jnp.take(product.reshape(tiles, run, channels, half), runs, axis=0)
    ids = jnp.take(target_half.reshape(tiles, run), runs, axis=0)
    arrived = lax.all_to_all(outgoing, "tile", split_axis=0, concat_axis=0, tiled=True)
    ids = lax.all_to_all(ids, "tile", split_axis=0, concat_axis=0, tiled=True).reshape(slots)
    selector = (jnp.arange(2 * blocks, dtype=jnp.int32)[:, None] == ids[None, :]).astype(BF16)
    sums = jnp.einsum(
        "hs,soa->hoa",
        selector,
        arrived.reshape(slots, channels, half),
        preferred_element_type=F32,
    ).astype(BF16)
    cells = sums.reshape(blocks, 2, channels, half).transpose(0, 2, 1, 3)
    cells = cells.reshape(blocks, channels, 2 * half)[:, :, np.array(lane_order())]
    cells = jnp.pad(cells, ((0, 0), (0, padded - channels), (0, 0)))
    even, odd = cells[0::2], cells[1::2]
    count = blocks // 2
    edges = jnp.concatenate([even[:count, :, :64], odd[:, :, :64]], axis=2)
    middle = jnp.concatenate([odd[:, :, 64:128], even[:count, :, 64:128]], axis=2)
    rows = jnp.concatenate(
        [edges, even[count:, :, :128], middle, even[:, :, 128:], odd[:, :, 128:]], axis=0
    )
    rows = rows.reshape(-1, half)
    pieces = [[rows[first:last]] for first, last in piece_rows(blocks, padded)]
    return pieces, prepare(rows)


def per_device(
    latlon_grad,
    remap_weight,
    src_block,
    owner,
    target_half,
    live_count,
    conv_weight,
    nbr_block,
    nbr_code,
):
    channels = latlon_grad.shape[1]
    hidden = conv_weight.shape[2]
    blocks = nbr_block.shape[0]
    padded = 8 * ((channels + 7) // 8)
    run = remap_weight.shape[0] // lax.axis_size("tile")
    small = lax.axis_size("tile") == 4 and run >= 2 * blocks
    gather = summed_here if small else summed_there
    ready = functools.partial(prepare, conv_weight, nbr_block, nbr_code, padded)
    pieces, (weight, rim_weight, pick) = gather(
        ready,
        latlon_grad,
        remap_weight,
        src_block,
        owner,
        target_half,
        live_count,
        blocks,
        padded,
    )
    lead, edges = sum_parts(pieces[0], (blocks + 1) // 2 * padded)
    pieces[0] = [lead]
    count = lax.axis_size(("tile", "chan"))
    near = [(source, (source + 1) % count) for source in range(count)]
    far = [(source, (source - 1) % count) for source in range(count)]
    arrived = [lax.ppermute(edges, ("tile", "chan"), pairs) for pairs in (near, far)]
    incoming = incoming_rims(
        (arrived[0], edges, arrived[1]), rim_weight, pick, blocks, padded
    )
    grads = convolve(pieces, weight, incoming, blocks, padded)
    return grads.transpose(1, 0, 2)


def solution(mesh):
    in_specs = (
        P(("member", "tile", "chan"), None, None),
        P(("tile", "chan"), None, None),
        P(("tile", "chan")),
        P(("tile", "chan")),
        P(("tile", "chan")),
        P(("tile", "chan")),
        P(),
        P(("tile", "chan"), None),
        P(("tile", "chan"), None),
    )
    out_specs = P(None, ("member", "tile", "chan"), None)
    return jax.shard_map(
        per_device, mesh=mesh, in_specs=in_specs, out_specs=out_specs, check_vma=False
    )
```

```python
import functools

import jax
import jax.numpy as jnp
import numpy as np
from jax import lax
from jax.experimental import pallas as pl
from jax.experimental.pallas import tpu as pltpu
from jax.sharding import PartitionSpec as P

BF16 = jnp.bfloat16
F32 = jnp.float32
SIDE = 16
CELLS = SIDE * SIDE
LANES = 128
TAPS = 9
VMEM_LIMIT = 48 * 1024 * 1024
SHARES = (6, 5, 3)


def edge_cell(side, position):
    return (
        position,
        SIDE * position,
        SIDE * (SIDE - 1) + position,
        SIDE * position + SIDE - 1,
    )[side]


def lane_order():
    edges = sorted({edge_cell(side, position) for side in range(4) for position in range(SIDE)})
    inner = [cell for cell in range(CELLS) if cell not in set(edges)]
    return edges + inner


def permutation_matrix():
    order = lane_order()
    matrix = np.zeros((CELLS, CELLS), np.float32)
    for lane, cell in enumerate(order):
        matrix[cell, lane] = 1
    return matrix


def shift_matrices():
    order = lane_order()
    matrix = np.zeros((TAPS, CELLS, CELLS), np.float32)
    for tap in range(TAPS):
        down, right = tap // 3 - 1, tap % 3 - 1
        for lane, cell in enumerate(order):
            row, column = cell // SIDE + down, cell % SIDE + right
            if 0 <= row < SIDE and 0 <= column < SIDE:
                matrix[tap, lane, row * SIDE + column] = 1
    return matrix


def edge_matrix(pairs):
    lane_of = {cell: lane for lane, cell in enumerate(lane_order())}
    matrix = np.zeros((pairs, 2, 64, 3, 4, pairs, 2, SIDE), np.float32)
    for shift in (-1, 0, 1):
        for side in range(4):
            for position in range(SIDE):
                if 0 <= position - shift < SIDE:
                    lane = lane_of[edge_cell(side, position - shift)]
                    for pair in range(pairs):
                        for half in range(2):
                            matrix[pair, half, lane, shift + 1, side, pair, half, position] = 1
    return matrix.reshape(pairs * LANES, 12 * 2 * SIDE * pairs)


def place_matrix():
    matrix = np.zeros((4, SIDE, CELLS), np.float32)
    for side in range(4):
        for position in range(SIDE):
            matrix[side, position, edge_cell(side, position)] = 1
    return matrix.reshape(4 * SIDE, CELLS)


def rim_taps(side):
    return [((0 + d), 3 * d, 6 + d, 3 * d + 2)[side] for d in range(3)]


def pack_matrices():
    even = permutation_matrix()
    odd = np.concatenate([even[:, 64:128], even[:, :64], even[:, 128:]], axis=1)
    return np.stack([even, odd])


def constant(matrix):
    return jnp.asarray(matrix, BF16)


def whole(array):
    rank = array.ndim
    return pl.BlockSpec(array.shape, lambda *_: (0,) * rank)


def piece_rows(blocks, padded):
    tiles = 2 * blocks
    shares = [sum(SHARES[:index]) for index in range(len(SHARES) + 1)]
    cuts = [-(-tiles * share // shares[-1]) for share in shares]
    cuts[1] = max(cuts[1], (blocks + 1) // 2)
    return [(first * padded, last * padded) for first, last in zip(cuts[:-1], cuts[1:])]


def remap_runs(
    flips,
    kind,
    latlon_grad,
    remap_weight,
    src_block,
    owner,
    target_half,
    live_count,
    blocks,
    padded,
    after=(),
):
    slots, half = remap_weight.shape[:2]
    channels = latlon_grad.shape[1]
    sources = latlon_grad.shape[0]
    tiles = lax.axis_size("tile")
    run = slots // tiles
    count = len(flips)
    halves = 2 * blocks
    odds = blocks // 2
    pieces = piece_rows(blocks, padded)
    cuts = [0, run // 2] + [run * (index + 1) for index in range(count)]

    def kernel(*refs):
        live, src_in, tgt_in, own_in, grad_in, weight_in, pack_in = refs[:7]
        refs = refs[7 + len(after) :]
        out_refs, refs = refs[: len(pieces)], refs[len(pieces) :]
        src, tgt, own, packed, grad, weight, pack, total, small_sem, weight_sem = refs
        tile = lax.axis_index("tile")
        small = [
            pltpu.make_async_copy(source, target, small_sem.at[index])
            for index, (source, target) in enumerate(
                (
                    (own_in, own),
                    (src_in, src),
                    (tgt_in, tgt),
                    (grad_in, packed),
                    (pack_in, pack),
                )
            )
        ]
        for copy in small[:4]:
            copy.start()
        small[0].wait()
        firsts = []
        for flip in flips:
            wanted = lax.bitwise_xor(tile, flip)
            found = jnp.int32(0)
            for index in range(tiles):
                found = found + jnp.where(own[index * run] == wanted, index, 0)
            firsts.append(found * run)
        large = []
        for part, (start, stop) in enumerate(zip(cuts[:-1], cuts[1:])):
            first = firsts[start // run] + start % run
            large.append(
                pltpu.make_async_copy(
                    weight_in.at[pl.ds(first, stop - start)],
                    weight.at[pl.ds(start, stop - start)],
                    weight_sem.at[part],
                )
            )
            large[-1].start()
        small[4].start()
        total[...] = jnp.zeros_like(total)
        for copy in small[1:4]:
            copy.wait()
        wide = packed[...].astype(F32)
        for source in range(sources):
            grad[source] = wide[:, source].astype(BF16)
        lane = lax.broadcasted_iota(jnp.int32, (odds * padded, half), 1)
        for part, (start, stop) in enumerate(zip(cuts[:-1], cuts[1:])):
            if part == 0 or start % run:
                large[part].wait()
            index = start // run
            for slot in range(start, stop):
                entry = firsts[index] + slot % run
                where = jnp.where(entry < live[0], tgt[entry], halves)
                total[index, where, :channels, :] += jnp.dot(
                    grad[src[entry]], weight[slot], preferred_element_type=F32
                )
            if stop % run:
                continue
            if index == 0:
                small[4].wait()
            if index + 1 < count:
                large[part + 1].wait()
            moved = []
            for parity in range(2):
                joined = jnp.concatenate(
                    [
                        jnp.concatenate(
                            [total[index, 2 * block], total[index, 2 * block + 1]], axis=1
                        )
                        for block in range(parity, blocks, 2)
                    ],
                    axis=0,
                )
                moved.append(
                    jnp.dot(joined.astype(BF16), pack[parity], preferred_element_type=F32)
                )
            both = odds * padded
            edges = jnp.where(lane < 64, moved[0][:both, :half], moved[1][:, :half])
            middle = jnp.where(lane < 64, moved[1][:, :half], moved[0][:both, :half])
            rows = jnp.concatenate(
                [
                    edges,
                    moved[0][both:, :half],
                    middle,
                    moved[0][:, half:],
                    moved[1][:, half:],
                ],
                axis=0,
            )
            for ref, (first, last) in zip(out_refs, pieces):
                ref[index] = rows[first:last].astype(kind)

    operands = [
        pltpu.with_memory_space_constraint(operand, pltpu.HBM)
        for operand in (
            src_block,
            target_half,
            owner,
            latlon_grad.transpose(1, 0, 2),
            remap_weight,
            constant(pack_matrices()),
        )
    ]
    return pl.pallas_call(
        kernel,
        in_specs=[pl.BlockSpec(memory_space=pltpu.SMEM)]
        + [pl.BlockSpec(memory_space=pltpu.HBM)] * 6
        + [pl.BlockSpec(memory_space=pl.ANY)] * len(after),
        out_specs=[pl.BlockSpec(memory_space=pltpu.VMEM)] * len(pieces),
        out_shape=[
            jax.ShapeDtypeStruct((count, last - first, half), kind) for first, last in pieces
        ],
        scratch_shapes=[
            pltpu.SMEM((slots,), jnp.int32),
            pltpu.SMEM((slots,), jnp.int32),
            pltpu.SMEM((slots,), jnp.int32),
            pltpu.VMEM((channels, sources, half), BF16),
            pltpu.VMEM((sources, channels, half), BF16),
            pltpu.VMEM((count * run, half, half), BF16),
            pltpu.VMEM((2, 2 * half, 2 * half), BF16),
            pltpu.VMEM((count, halves + 1, padded, half), F32),
            pltpu.SemaphoreType.DMA((5,)),
            pltpu.SemaphoreType.DMA((len(cuts) - 1,)),
        ],
        compiler_params=pltpu.CompilerParams(vmem_limit_bytes=VMEM_LIMIT),
        name="remap",
    )(live_count, *operands, *after)


def add_halves(kept, arrived, after=()):
    def kernel(kept_ref, arrived_ref, *refs):
        here_ref, there_ref = refs[len(after) :]
        here_ref[...] = kept_ref[0] + arrived_ref[0].astype(F32)
        there_ref[...] = (kept_ref[1] + arrived_ref[1].astype(F32)).astype(BF16)

    vmem = pl.BlockSpec(memory_space=pltpu.VMEM)
    return pl.pallas_call(
        kernel,
        in_specs=[vmem] * 2 + [pl.BlockSpec(memory_space=pl.ANY)] * len(after),
        out_specs=[vmem] * 2,
        out_shape=[
            jax.ShapeDtypeStruct(kept.shape[1:], F32),
            jax.ShapeDtypeStruct(kept.shape[1:], BF16),
        ],
        compiler_params=pltpu.CompilerParams(vmem_limit_bytes=VMEM_LIMIT),
        name="add_halves",
    )(kept, arrived, *after)


def sum_parts(parts, edge_rows):
    def kernel(*refs):
        total = refs[0][...].astype(F32)
        for ref in refs[1:-2]:
            total = total + ref[...].astype(F32)
        total = total.astype(BF16)
        refs[-2][...] = total
        refs[-1][...] = total[:edge_rows]

    return pl.pallas_call(
        kernel,
        out_shape=[
            jax.ShapeDtypeStruct(parts[0].shape, BF16),
            jax.ShapeDtypeStruct((edge_rows, parts[0].shape[1]), BF16),
        ],
        compiler_params=pltpu.CompilerParams(vmem_limit_bytes=VMEM_LIMIT),
        name="sum_parts",
    )(*parts)


def split_rows(padded):
    full = 16 * (padded // 16)
    return full, 16 * ((TAPS * (padded - full) + 15) // 16)


def prepare(conv_weight, nbr_block, nbr_code, padded, after):
    taps, channels, hidden = conv_weight.shape
    blocks = nbr_block.shape[0]
    pairs = (blocks + 1) // 2
    devices = lax.axis_size(("tile", "chan"))
    span = 2 * SIDE * pairs
    columns = 4 * 3 * span
    slots = blocks * 4 * SIDE
    full, rest = split_rows(padded)

    def kernel(nbr, code, taps_ref, unread, weight_ref, rim_ref, pick_ref):
        me = lax.axis_index(("tile", "chan"))
        empty = jnp.zeros((padded - channels, hidden), F32)
        rows = []
        for tap in range(taps):
            rows.append(jnp.concatenate([taps_ref[tap].astype(F32), empty], axis=0))
        tail = jnp.zeros((rest - taps * (padded - full), hidden), F32)
        lead = jnp.zeros((4 * SIDE, hidden), F32)
        stacked = [lead] + [row[:full] for row in rows] + [row[full:] for row in rows] + [tail]
        weight_ref[...] = jnp.concatenate(stacked, axis=0).T.astype(BF16)
        for side in range(4):
            chosen = [rows[tap] for tap in rim_taps(side)]
            rim_ref[side * hidden : (side + 1) * hidden] = (
                jnp.concatenate(chosen, axis=0).T.astype(BF16)
            )
        lane = lax.broadcasted_iota(jnp.int32, (1, slots), 1)
        which = lane // SIDE
        position = lane % SIDE
        start = jnp.zeros((1, slots), jnp.int32)
        turned = jnp.zeros((1, slots), jnp.int32)
        for block in range(blocks):
            for side in range(4):
                other = nbr[side, block]
                turn = code[side, block]
                relative = lax.rem(other // blocks - me + 1 + devices, devices)
                part = relative
                column = (turn // 2 * 3 + part) * span + lax.rem(other, blocks) * SIDE
                start = jnp.where(which == 4 * block + side, column, start)
                turned = jnp.where(which == 4 * block + side, turn % 2, turned)
        source = start + jnp.where(turned == 1, SIDE - 1 - position, position)
        row = lax.broadcasted_iota(jnp.int32, (columns, slots), 0)
        pick_ref[...] = jnp.where(row == source, 1.0, 0.0).astype(BF16)

    smem = pl.BlockSpec(memory_space=pltpu.SMEM)
    vmem = pl.BlockSpec(memory_space=pltpu.VMEM)
    return pl.pallas_call(
        kernel,
        in_specs=[smem, smem, vmem, pl.BlockSpec(memory_space=pl.ANY)],
        out_specs=[vmem] * 3,
        out_shape=[
            jax.ShapeDtypeStruct((hidden, 4 * SIDE + taps * full + rest), BF16),
            jax.ShapeDtypeStruct((4 * hidden, 3 * padded), BF16),
            jax.ShapeDtypeStruct((columns, slots), BF16),
        ],
        compiler_params=pltpu.CompilerParams(vmem_limit_bytes=VMEM_LIMIT),
        name="prepare",
    )(nbr_block.T, nbr_code.T, conv_weight, after)


def incoming_rims(edges, rim_weight, pick, blocks, padded):
    pairs = (blocks + 1) // 2
    span = 2 * SIDE * pairs
    hidden = rim_weight.shape[0] // 4
    slots = pick.shape[1]

    def kernel(near_ref, own_ref, far_ref, weight_ref, pick_ref, edge_ref, out_ref):
        rows = []
        for ref in (near_ref, own_ref, far_ref):
            edges = ref[...].astype(F32)
            rows.append(
                jnp.concatenate(
                    [edges[pair * padded : (pair + 1) * padded] for pair in range(pairs)], axis=1
                )
            )
        shifted = jnp.dot(
            jnp.concatenate(rows, axis=0).astype(BF16),
            edge_ref[...],
            preferred_element_type=F32,
        )
        rims = []
        for side in range(4):
            stack = jnp.concatenate(
                [
                    jnp.concatenate(
                        [
                            shifted[
                                device * padded : (device + 1) * padded,
                                (4 * shift + side) * span : (4 * shift + side + 1) * span,
                            ]
                            for device in range(3)
                        ],
                        axis=1,
                    )
                    for shift in range(3)
                ],
                axis=0,
            ).astype(BF16)
            rims.append(
                jnp.dot(
                    weight_ref[side * hidden : (side + 1) * hidden],
                    stack,
                    preferred_element_type=F32,
                ).astype(BF16)
            )
        out_ref[:, :slots] = jnp.dot(
            jnp.concatenate(rims, axis=1), pick_ref[...], preferred_element_type=F32
        ).astype(BF16)

    return pl.pallas_call(
        kernel,
        out_shape=jax.ShapeDtypeStruct((hidden, pairs * LANES), BF16),
        compiler_params=pltpu.CompilerParams(vmem_limit_bytes=VMEM_LIMIT),
        name="rims",
    )(*edges, rim_weight, pick, constant(edge_matrix(pairs)))


def convolve(pieces, weight, incoming, blocks, padded):
    hidden = weight.shape[0]
    flat = [part for piece in pieces for part in piece]
    parts = len(flat)
    full, rest = split_rows(padded)
    evens, odds = (blocks + 1) // 2, blocks // 2
    order = [*range(0, blocks, 2), *range(1, blocks, 2)]

    def kernel(*refs):
        part_refs = list(refs[:parts])
        weight_ref, incoming_ref, shift_ref, place_ref = refs[parts : 4 + parts]
        out_ref, stack, result, sems = refs[4 + parts :]
        copies = []
        totals = []
        for piece in pieces:
            total = part_refs.pop(0)[...].astype(F32)
            for _ in piece[1:]:
                total = total + part_refs.pop(0)[...].astype(F32)
            totals.append(total)
        total = jnp.concatenate(totals, axis=0)
        edge_rows, both = evens * padded, odds * padded
        edge, middle = total[:both], total[edge_rows : edge_rows + both]
        lane = lax.broadcasted_iota(jnp.int32, (both, LANES), 1)
        even = jnp.where(lane < 64, edge, middle)
        odd = pltpu.roll(jnp.where(lane < 64, middle, edge), 64, 1)
        lead = jnp.concatenate([even, total[both:edge_rows], odd], axis=0)
        cells = jnp.concatenate([lead, total[edge_rows + both :]], axis=1).astype(BF16)
        rests = []
        for tap in range(TAPS):
            moved = jnp.dot(cells, shift_ref[tap], preferred_element_type=F32)
            moved = moved.reshape(blocks, padded, CELLS)
            first = 4 * SIDE + full * tap
            stack[:, first : first + full, :] = moved[:, :full].astype(BF16)
            rests.append(moved[:, full:])
        rests.append(jnp.zeros((blocks, rest - TAPS * (padded - full), CELLS), F32))
        stack[:, 4 * SIDE + full * TAPS :, :] = jnp.concatenate(rests, axis=1).astype(BF16)
        lane = lax.broadcasted_iota(jnp.int32, (hidden, LANES), 1)
        for index, block in enumerate(order):
            stack[index, : 4 * SIDE, :] = place_ref[...]
            pair = incoming_ref[:, LANES * (block // 2) : LANES * (block // 2 + 1)].astype(F32)
            if block % 2:
                pair = pltpu.roll(pair, 64, 1)
            ahead = jnp.where(lane < 4 * SIDE, pair, weight_ref[:, :LANES].astype(F32))
            mixed = jnp.concatenate([ahead.astype(BF16), weight_ref[:, LANES:]], axis=1)
            grad = jnp.dot(mixed, stack[index], preferred_element_type=F32)
            result[block] = grad.astype(BF16)
            copies.append(
                pltpu.make_async_copy(result.at[block], out_ref.at[block], sems.at[block])
            )
            copies[-1].start()
        for copy in copies:
            copy.wait()

    return pl.pallas_call(
        kernel,
        out_shape=jax.ShapeDtypeStruct((blocks, hidden, CELLS), BF16),
        out_specs=pl.BlockSpec(memory_space=pltpu.HBM),
        scratch_shapes=[
            pltpu.VMEM((blocks, 4 * SIDE + TAPS * full + rest, CELLS), BF16),
            pltpu.VMEM((blocks, hidden, CELLS), BF16),
            pltpu.SemaphoreType.DMA((blocks,)),
        ],
        compiler_params=pltpu.CompilerParams(vmem_limit_bytes=VMEM_LIMIT),
        name="convolve",
    )(
        *flat,
        weight,
        incoming,
        constant(shift_matrices()),
        constant(place_matrix()),
    )


def swapped(value, flip):
    pairs = [(source, source ^ flip) for source in range(lax.axis_size("tile"))]
    return lax.ppermute(value, "tile", pairs)


def summed_here(
    prepare, latlon_grad, remap_weight, src_block, owner, target_half, live_count, blocks, padded
):
    operands = (
        latlon_grad, remap_weight, src_block, owner, target_half, live_count, blocks, padded
    )
    moving = list(remap_runs((1, 3), BF16, *operands))
    kept = remap_runs((0, 2), F32, *operands, (moving[0],))
    pieces = []
    for index, stays in enumerate(kept):
        stays, leaves = add_halves(stays, swapped(moving[index], 1))
        if index == 0:
            weight, *ready = prepare(leaves)
            weight, moving[-1] = lax.optimization_barrier((weight, moving[-1]))
        pieces.append([stays, swapped(leaves, 2)])
    return pieces, (weight, *ready)


def summed_there(
    prepare, latlon_grad, remap_weight, src_block, owner, target_half, live_count, blocks, padded
):
    slots, half = remap_weight.shape[:2]
    channels = latlon_grad.shape[1]
    tiles = lax.axis_size("tile")
    run = slots // tiles
    live = jnp.arange(slots, dtype=jnp.int32) < live_count[0]
    runs = jnp.argsort(owner.reshape(tiles, run)[:, 0])
    picked = jnp.take(latlon_grad, src_block, axis=0)
    product = jnp.einsum("eoa,eab->eob", picked, remap_weight, preferred_element_type=F32)
    product = jnp.where(live[:, None, None], product, 0).astype(BF16)
    outgoing = jnp.take(product.reshape(tiles, run, channels, half), runs, axis=0)
    ids = jnp.take(target_half.reshape(tiles, run), runs, axis=0)
    arrived = lax.all_to_all(outgoing, "tile", split_axis=0, concat_axis=0, tiled=True)
    ids = lax.all_to_all(ids, "tile", split_axis=0, concat_axis=0, tiled=True).reshape(slots)
    selector = (jnp.arange(2 * blocks, dtype=jnp.int32)[:, None] == ids[None, :]).astype(BF16)
    sums = jnp.einsum(
        "hs,soa->hoa",
        selector,
        arrived.reshape(slots, channels, half),
        preferred_element_type=F32,
    ).astype(BF16)
    cells = sums.reshape(blocks, 2, channels, half).transpose(0, 2, 1, 3)
    cells = cells.reshape(blocks, channels, 2 * half)[:, :, np.array(lane_order())]
    cells = jnp.pad(cells, ((0, 0), (0, padded - channels), (0, 0)))
    even, odd = cells[0::2], cells[1::2]
    count = blocks // 2
    edges = jnp.concatenate([even[:count, :, :64], odd[:, :, :64]], axis=2)
    middle = jnp.concatenate([odd[:, :, 64:128], even[:count, :, 64:128]], axis=2)
    rows = jnp.concatenate(
        [edges, even[count:, :, :128], middle, even[:, :, 128:], odd[:, :, 128:]], axis=0
    )
    rows = rows.reshape(-1, half)
    pieces = [[rows[first:last]] for first, last in piece_rows(blocks, padded)]
    return pieces, prepare(rows)


def per_device(
    latlon_grad,
    remap_weight,
    src_block,
    owner,
    target_half,
    live_count,
    conv_weight,
    nbr_block,
    nbr_code,
):
    channels = latlon_grad.shape[1]
    hidden = conv_weight.shape[2]
    blocks = nbr_block.shape[0]
    padded = 8 * ((channels + 7) // 8)
    run = remap_weight.shape[0] // lax.axis_size("tile")
    small = lax.axis_size("tile") == 4 and run >= 2 * blocks
    gather = summed_here if small else summed_there
    ready = functools.partial(prepare, conv_weight, nbr_block, nbr_code, padded)
    pieces, (weight, rim_weight, pick) = gather(
        ready,
        latlon_grad,
        remap_weight,
        src_block,
        owner,
        target_half,
        live_count,
        blocks,
        padded,
    )
    lead, edges = sum_parts(pieces[0], (blocks + 1) // 2 * padded)
    pieces[0] = [lead]
    count = lax.axis_size(("tile", "chan"))
    near = [(source, (source + 1) % count) for source in range(count)]
    far = [(source, (source - 1) % count) for source in range(count)]
    arrived = [lax.ppermute(edges, ("tile", "chan"), pairs) for pairs in (near, far)]
    incoming = incoming_rims(
        (arrived[0], edges, arrived[1]), rim_weight, pick, blocks, padded
    )
    grads = convolve(pieces, weight, incoming, blocks, padded)
    return grads.transpose(1, 0, 2)


def solution(mesh):
    in_specs = (
        P(("member", "tile", "chan"), None, None),
        P(("tile", "chan"), None, None),
        P(("tile", "chan")),
        P(("tile", "chan")),
        P(("tile", "chan")),
        P(("tile", "chan")),
        P(),
        P(("tile", "chan"), None),
        P(("tile", "chan"), None),
    )
    out_specs = P(None, ("member", "tile", "chan"), None)
    return jax.shard_map(
        per_device, mesh=mesh, in_specs=in_specs, out_specs=out_specs, check_vma=False
    )
```
